32 devices in a mesh: sp: 8 (over y, x, core), tp: 4 (over z).
Axes of the slice: x: 2, y: 2, z: 4, core: 2. Of those that a mesh axis runs over, the one named last changes fastest.
Arguments:
- state: bfloat16 [10, 96, 138240], P(None, 'sp', 'tp'), may hold values from -6 to 6
- cotangent: bfloat16 [10, 96, 138240], P(None, 'sp', 'tp'), may hold values from -6 to 6
- rollout_lengths: int32 [2], replicated, may hold values from 1 to 5, as said below
- channel_sizes: int32 [4], replicated, may hold values from 160 to 161, as said below
- owner_slots: int32 [94], replicated, may hold values from 0 to 95, as said below
- master: float32 [96, 768, 768], P('sp', 'tp')
- first_moment: float32 [96, 768, 768], P('sp', 'tp')
- second_moment: float32 [96, 768, 768], P('sp', 'tp'), as said below
- gains: float32 [2, 768], P(None, 'tp'), may hold values from 0.5 to 1.5
- gain_first: float32 [2, 768], P(None, 'tp'), may hold values from -2048 to 2048
- gain_second: float32 [2, 768], P(None, 'tp'), may hold values from 103680 to 414720
Outputs:
- block_out: bfloat16 [10, 96, 138240], P(None, 'sp', 'tp')
- grad_state: bfloat16 [10, 96, 138240], P(None, 'sp', 'tp')
- new_master: float32 [96, 768, 768], P('sp', 'tp')
- new_copy: bfloat16 [96, 768, 768], P('sp', 'tp')
- new_first: float32 [96, 768, 768], P('sp', 'tp')
- new_second: float32 [96, 768, 768], P('sp', 'tp')
- new_gains: float32 [2, 768], P(None, 'tp')
- new_gain_first: float32 [2, 768], P(None, 'tp')
- new_gain_second: float32 [2, 768], P(None, 'tp')
The draws below stay inside these ranges and needn't reach their ends.
Inputs may be any that keep to these rules, and one draw needn't show every extreme that they name: `rollout_lengths`: some sample has exactly 5 steps. `channel_sizes`: they sum to 641. `owner_slots`: distinct; slot q lies on sp index q div 12; some sp index owns 12 pieces. `second_moment`: positive.
All inputs are finite; a program needn't handle non-finite values.
Results may differ from the reference program's by a relative error of at most 0.015.
Values may be sent and summed in bfloat16 or wider, within the bound.
No kernel may reach another device: no remote copies, remote signals or barrier semaphores. Data moves between devices by JAX's collectives and lax.ppermute only.
A program may use at most 832 MiB of HBM per device.

```python
import math
import jax
import jax.numpy as jnp
from jax import lax

CH = 641
NLAT = 90
NLON = 180
MMAX = 90
ROLL = 5
SAMPLES = 2
CSH = 192
CHANNEL_SPOTS = 768
HSH = 384
HP = 1536
SLOTS = 10
NLATP = 96
MP = 96
WEIGHT_PIECES = 94
OWN = 12
OWNER_SLOTS = 96
N_SP = 8
N_TP = 4


def owner_table(key):
    base = jax.random.fold_in(key, 11)
    key_dev, key_sequence, key_assign = jax.random.split(base, 3)
    full_dev = jax.random.randint(key_dev, (), 0, N_SP)
    ranking = jax.random.permutation(key_sequence, OWNER_SLOTS)
    rank = jnp.argsort(ranking)
    slot_numbers = jnp.arange(OWNER_SLOTS)
    score = jnp.where(slot_numbers // OWN == full_dev, slot_numbers % OWN, OWN + rank)
    chosen = jnp.argsort(score)[:WEIGHT_PIECES]
    return chosen[jax.random.permutation(key_assign, WEIGHT_PIECES)].astype(jnp.int32)


def slot_scales(key):
    holder_list = owner_table(key)
    weight_piece = jnp.full((OWNER_SLOTS,), -1, jnp.int32).at[holder_list].set(jnp.arange(WEIGHT_PIECES).astype(jnp.int32))
    weight_scale = jnp.where(weight_piece >= MMAX + 2, (2.0 * CH) ** (-0.5), CH ** (-0.5)).astype(jnp.float32)
    grad_spec = 1.2 * (SLOTS * MMAX) ** 0.5
    grad_in = 0.4 * (SLOTS * NLAT * NLON) ** 0.5
    grad_out = 0.5 * (SLOTS * NLAT * NLON) ** 0.5
    grad_scale = jnp.where(weight_piece < MMAX, grad_spec, jnp.where(weight_piece < MMAX + 2, grad_in, grad_out)).astype(jnp.float32)
    return (weight_scale, grad_scale)


def draw_rollout_lengths(key, part):
    key_len, key_pick = jax.random.split(jax.random.fold_in(key, 31))
    lengths = jax.random.randint(key_len, (SAMPLES,), 1, ROLL + 1)
    pick = jax.random.randint(key_pick, (), 0, SAMPLES)
    return lengths.at[pick].set(ROLL).astype(jnp.int32)


def draw_channel_sizes(key, part):
    perm = jax.random.permutation(jax.random.fold_in(key, 41), N_TP)
    return (CH // N_TP + (perm < CH % N_TP).astype(jnp.int32)).astype(jnp.int32)


def draw_owner_slots(key, part):
    return owner_table(key)


def draw_master(key, part):
    weight_scale, grad_scale = slot_scales(key)
    value_entries = jax.random.normal(jax.random.fold_in(key, 21), (OWNER_SLOTS, CHANNEL_SPOTS, CHANNEL_SPOTS), jnp.float32)
    return value_entries * weight_scale[:, None, None]


def draw_first_moment(key, part):
    weight_scale, grad_scale = slot_scales(key)
    value_entries = jax.random.normal(jax.random.fold_in(key, 22), (OWNER_SLOTS, CHANNEL_SPOTS, CHANNEL_SPOTS), jnp.float32)
    return value_entries * grad_scale[:, None, None]


def draw_second_moment(key, part):
    weight_scale, grad_scale = slot_scales(key)
    multiplier = jnp.exp(jax.random.uniform(jax.random.fold_in(key, 23), (OWNER_SLOTS, CHANNEL_SPOTS, CHANNEL_SPOTS), jnp.float32, 0.0, math.log(4.0)))
    return multiplier * (grad_scale * grad_scale)[:, None, None]


def steps_of(stream_key, shape, cuts, smallest, largest):
    level = 1.0
    for position, shards_of in cuts:
        steps = jax.random.uniform(jax.random.fold_in(jax.random.fold_in(stream_key, 6), position), (shards_of,), jnp.float32, smallest / len(cuts), largest / len(cuts))
        level = level * jnp.repeat(jnp.exp(steps), shape[position] // shards_of).reshape((-1,) + (1,) * (len(shape) - 1 - position))
    return level


def centred(rng, dims, scale, reach, cuts=(), kind=jnp.bfloat16):
    level = steps_of(rng, dims, cuts, -0.22, 0.18) if cuts else 1.0
    result = jax.random.normal(rng, dims, jnp.float32) * scale * level
    return jnp.minimum(jnp.maximum(result, -reach), reach).astype(kind)


def setup_inputs(seed: int = 0) -> dict:
    key_list = jax.random.split(jax.random.key(seed), 12)
    return {
        "state": centred(key_list[0], (SLOTS, NLATP, CHANNEL_SPOTS * NLON), 1.0, 6.0, ((1, 8), (2, 4))),
        "cotangent": centred(key_list[1], (SLOTS, NLATP, CHANNEL_SPOTS * NLON), 1.0, 6.0, ((1, 8), (2, 4))),
        "rollout_lengths": draw_rollout_lengths(jax.random.fold_in(key_list[11], 71), 0),
        "channel_sizes": draw_channel_sizes(jax.random.fold_in(key_list[11], 71), 0),
        "owner_slots": draw_owner_slots(jax.random.fold_in(key_list[11], 71), 0),
        "master": draw_master(jax.random.fold_in(key_list[11], 71), 0),
        "first_moment": draw_first_moment(jax.random.fold_in(key_list[11], 71), 0),
        "second_moment": draw_second_moment(jax.random.fold_in(key_list[11], 71), 0),
        "gains": jnp.clip(1.0 + 0.1 * jax.random.normal(key_list[8], (2, CHANNEL_SPOTS), jnp.float32), 0.5, 1.5),
        "gain_first": centred(key_list[9], (2, CHANNEL_SPOTS), (0.8 * (SLOTS * NLAT * NLON) ** 0.5), 2048.0, ((1, 4),), jnp.float32),
        "gain_second": jnp.clip(jnp.exp(math.log(414720.0) - 1.3862944 * jax.random.uniform(key_list[10], (2, CHANNEL_SPOTS), jnp.float32) ** steps_of(key_list[10], (2, CHANNEL_SPOTS), ((1, 4),), -0.2, 0.2)), 103680.0, 414720.0),
    }


@jax.custom_vjp
def low(v):
    return lax.optimization_barrier(v.astype(jnp.bfloat16)).astype(jnp.float32)

@jax.custom_vjp
def low_back(v):
    return v

def low_keep(v):
    return (low(v), None)

def low_pass(kept, grad):
    return (grad,)

def back_keep(v):
    return (v, None)

def back_low(kept, grad):
    return (low(grad),)
low.defvjp(low_keep, low_pass)
low_back.defvjp(back_keep, back_low)
EPS = 1e-05
ADAM_EPS = 1e-08
BIAS_FIX = 1.0 - 0.5 ** 5
HI = lax.Precision.HIGHEST

def gelu_tanh(value):
    return jax.nn.gelu(value, approximate=True)

def tables(nlat, nlatp, nlon, mmax, mpad):
    rows = jnp.arange(nlat).astype(jnp.float32)
    theta = (rows + 0.5) * (math.pi / nlat)
    cosine = jnp.cos(theta)
    sine = jnp.sin(theta)
    orders = jnp.arange(mmax).astype(jnp.float32)
    steps = jnp.arange(1, mmax).astype(jnp.float32)
    logs = 0.5 * jnp.log((2.0 * steps + 1.0) / (2.0 * steps))
    logcum = jnp.concatenate([jnp.zeros((1,), jnp.float32), jnp.cumsum(logs)])
    diagonal = jnp.exp(0.5 * math.log(0.5) + logcum[:, None] + orders[:, None] * jnp.log(sine)[None, :])
    col = orders[:, None]

    def degree_step(carry, degree):
        prev_one, prev_two = carry
        sq = degree * degree
        coef_a = jnp.sqrt(jnp.maximum(4.0 * sq - 1.0, 0.0) / jnp.maximum(sq - col * col, 1.0))
        coef_b = jnp.sqrt(jnp.maximum((degree - 1.0) ** 2 - col * col, 0.0) / jnp.maximum(4.0 * (degree - 1.0) ** 2 - 1.0, 1.0))
        general = coef_a * (cosine[None, :] * prev_one - coef_b * prev_two)
        current = jnp.where(degree == col, diagonal, jnp.where(degree == col + 1.0, jnp.sqrt(2.0 * col + 3.0) * cosine[None, :] * prev_one, jnp.where(degree > col + 1.0, general, 0.0)))
        return ((current, prev_one), current)
    start = jnp.zeros((mmax, nlat), jnp.float32)
    _, legendre = lax.scan(degree_step, (start, start), orders)
    weights = sine * (math.pi / nlat)
    analysis = jnp.transpose(legendre, (1, 2, 0)) * weights[None, :, None]
    synthesis = jnp.transpose(legendre, (1, 0, 2))
    analysis = jnp.pad(analysis, ((0, mpad - mmax), (0, nlatp - nlat), (0, 0)))
    synthesis = jnp.pad(synthesis, ((0, mpad - mmax), (0, 0), (0, nlatp - nlat)))
    lon = jnp.arange(nlon).astype(jnp.int32)
    order_ids = jnp.arange(mmax).astype(jnp.int32)
    angle = (lon[:, None] * order_ids[None, :] % nlon).astype(jnp.float32) * (2.0 * math.pi / nlon)
    scale = math.sqrt(2.0 / nlon)
    fwd_basis = jnp.stack([jnp.cos(angle) * scale, -jnp.sin(angle) * scale], axis=1)
    half = jnp.where(order_ids == 0, 0.5, 1.0).astype(jnp.float32)
    inv_basis = jnp.transpose(fwd_basis, (1, 2, 0)) * half[None, :, None]
    fwd_basis = jnp.pad(fwd_basis, ((0, 0), (0, 0), (0, mpad - mmax)))
    inv_basis = jnp.pad(inv_basis, ((0, 0), (0, mpad - mmax), (0, 0)))
    return (fwd_basis.astype(jnp.bfloat16), analysis.astype(jnp.bfloat16), synthesis.astype(jnp.bfloat16), inv_basis.astype(jnp.bfloat16))

def reference(state, cotangent, rollout_lengths, channel_sizes, owner_slots, master, first_moment, second_moment, gains, gain_first, gain_second):
    fwd_basis, analysis, synthesis, inv_basis = [t.astype(jnp.float32) for t in tables(NLAT, NLATP, NLON, MMAX, MP)]
    chan = jnp.arange(CHANNEL_SPOTS).astype(jnp.int32)
    cmask = (chan % CSH < channel_sizes[chan // CSH]).astype(jnp.float32)
    hid = jnp.arange(HP).astype(jnp.int32)
    hmask = (hid % HSH < 2 * channel_sizes[hid // HSH]).astype(jnp.float32)
    lmask = (jnp.arange(NLATP).astype(jnp.int32) < NLAT).astype(jnp.float32)
    slot_numbers = jnp.arange(SLOTS).astype(jnp.int32)
    smask = (slot_numbers % ROLL < rollout_lengths[slot_numbers // ROLL]).astype(jnp.float32)

    def arrange(pair):
        return jnp.transpose(pair.reshape(2, N_TP, CSH, CHANNEL_SPOTS), (3, 1, 0, 2)).reshape(CHANNEL_SPOTS, HP)

    def forward(inputs, pieces, gain_vec):
        rounded = low(pieces)
        spec_w = jnp.transpose(rounded[:MMAX], (0, 2, 1)) * cmask[None, :, None] * cmask[None, None, :]
        w_in = arrange(rounded[MMAX:MMAX + 2]) * cmask[:, None] * hmask[None, :]
        w_out = arrange(rounded[MMAX + 2:MMAX + 4]) * cmask[:, None] * hmask[None, :]

        def slot_fn(one_slot):
            grid = jnp.transpose(one_slot.reshape(NLATP, CHANNEL_SPOTS, NLON), (0, 2, 1))
            x = grid * cmask * lmask[:, None, None]
            inv_one = lax.rsqrt(lax.optimization_barrier(jnp.sum(x * x, axis=-1, keepdims=True)) / CH + EPS)
            normed = low(x * inv_one * gain_vec[0])
            fourier = low_back(low(jnp.einsum('jnc,nkm->mjkc', normed, fwd_basis, precision=HI)))
            coef = low_back(low(jnp.einsum('mjkc,mjl->mklc', fourier, analysis, precision=HI)))
            mixed = low_back(low(jnp.einsum('mklc,lco->mklo', coef, spec_w, precision=HI)))
            synth = low_back(low(jnp.einsum('mklo,mlj->mjko', mixed, synthesis, precision=HI)))
            spec_out = low_back(jnp.einsum('mjko,kmn->jno', synth, inv_basis, precision=HI))
            resid = x + spec_out
            inv_two = lax.rsqrt(lax.optimization_barrier(jnp.sum(resid * resid, axis=-1, keepdims=True)) / CH + EPS)
            normed_two = low(resid * inv_two * gain_vec[1]).reshape(-1, CHANNEL_SPOTS)
            pre_act = low_back(jnp.dot(normed_two, w_in, precision=HI, preferred_element_type=jnp.float32))
            act = low(gelu_tanh(pre_act))
            mlp_out = low_back(jnp.dot(act, w_out.T, precision=HI, preferred_element_type=jnp.float32))
            out = resid + mlp_out.reshape(resid.shape)
            return jnp.transpose(out, (0, 2, 1)).reshape(NLATP, CHANNEL_SPOTS * NLON)
        return lax.map(jax.checkpoint(slot_fn), inputs)
    block, pull = jax.vjp(forward, state.astype(jnp.float32), master[owner_slots], gains)
    cot = cotangent.astype(jnp.float32) * smask[:, None, None]
    grad_in, grad_pieces, grad_gains = pull(cot)
    slot_grads = jnp.zeros(master.shape, jnp.float32).at[owner_slots].set(grad_pieces)
    new_first = 0.5 * first_moment + 0.5 * slot_grads
    new_second = 0.5 * second_moment + 0.5 * slot_grads * slot_grads
    update = new_first / BIAS_FIX / (jnp.sqrt(new_second / BIAS_FIX) + ADAM_EPS)
    new_master = master - 0.03 * (update + 0.01 * master)
    gain_one = 0.5 * gain_first + 0.5 * grad_gains
    gain_two = 0.5 * gain_second + 0.5 * grad_gains * grad_gains
    new_gains = gains - 0.5 * (gain_one / BIAS_FIX) / (jnp.sqrt(gain_two / BIAS_FIX) + ADAM_EPS)
    return (block.astype(jnp.bfloat16), grad_in.astype(jnp.bfloat16), new_master, new_master.astype(jnp.bfloat16), new_first, new_second, new_gains, gain_one, gain_two)
```

```python
import functools
import math

import jax
import jax.numpy as jnp
import ml_dtypes
import numpy as np
from jax import lax
from jax.experimental import pallas as pl
from jax.experimental.pallas import tpu as pltpu
from jax.sharding import PartitionSpec as P

CH = 641
CVALID = 161
NLAT = 90
ROLL = 5
EPS = 1e-05
ADAM_EPS = 1e-08
BIAS_FIX = 1.0 - 0.5**5
GELU_A = math.sqrt(2.0 / math.pi)
GELU_B = 0.044715
BF = jnp.bfloat16
F32 = jnp.float32
NT = (((1,), (1,)), ((), ()))
NN = (((1,), (0,)), ((), ()))
TN = (((0,), (0,)), ((), ()))


def mm(a, b, dims=NN):
    return lax.dot_general(a, b, dims, preferred_element_type=F32)


def tables(nlat, nlatp, nlon, mmax, mpad):
    theta = (np.arange(nlat) + 0.5) * (math.pi / nlat)
    cosine, sine = np.cos(theta), np.sin(theta)
    legendre = np.zeros((mmax, mmax, nlat))
    for m in range(mmax):
        value = math.sqrt(0.5) * np.ones(nlat)
        for k in range(1, m + 1):
            value = value * math.sqrt((2 * k + 1) / (2 * k)) * sine
        legendre[m, m] = value
        if m + 1 < mmax:
            legendre[m, m + 1] = math.sqrt(2 * m + 3) * cosine * value
        for l in range(m + 2, mmax):
            a = math.sqrt((4 * l * l - 1) / (l * l - m * m))
            b = math.sqrt(((l - 1) ** 2 - m * m) / (4 * (l - 1) ** 2 - 1))
            legendre[m, l] = a * (cosine * legendre[m, l - 1] - b * legendre[m, l - 2])
    analysis = np.zeros((mpad, mmax, nlatp))
    synthesis = np.zeros((mpad, mmax, nlatp))
    analysis[:mmax, :, :nlat] = legendre * sine * (math.pi / nlat)
    synthesis[:mmax, :, :nlat] = legendre
    angle = (np.arange(mmax)[:, None] * np.arange(nlon)[None, :] % nlon) * (2.0 * math.pi / nlon)
    fwd = np.zeros((mpad, 2, nlon))
    fwd[:mmax, 0] = np.cos(angle) * math.sqrt(2.0 / nlon)
    fwd[:mmax, 1] = -np.sin(angle) * math.sqrt(2.0 / nlon)
    fwd_low = fwd.astype(np.float32).astype(ml_dtypes.bfloat16)
    inv = fwd.copy()
    inv[0] *= 0.5
    inv_low = inv.astype(np.float32).astype(ml_dtypes.bfloat16)
    low = lambda v: v.astype(np.float32).astype(ml_dtypes.bfloat16)
    return (
        fwd_low.reshape(mpad * 2, nlon),
        inv_low.reshape(mpad * 2, nlon),
        low(analysis),
        low(synthesis),
    )


def params(mib):
    return pltpu.CompilerParams(vmem_limit_bytes=mib * 2**20)


def whole(shape):
    return pl.BlockSpec(shape, lambda *_: (0,) * len(shape), pipeline_mode=pl.Buffered(1))


SMEM = pl.BlockSpec(memory_space=pltpu.SMEM)


LANE = 128


def spread(scr, start, value):
    rows, cols = value.shape
    for t in range(cols // LANE):
        scr[t, start : start + rows, :] = value[:, t * LANE : (t + 1) * LANE].astype(F32)


def pick_rows(scr, start, count, stride):
    parts = [scr[t, pl.ds(start, count, stride=stride), :] for t in range(scr.shape[0])]
    return jnp.concatenate(parts, axis=1).astype(BF)


def pack_rows(state, n_tp, each, lanes, tile):
    slots, latd, _ = state.shape

    def body(x_ref, o_ref):
        d = pl.program_id(0)
        parts = []
        for i in range(each):
            v = x_ref[i].astype(F32)
            parts.append(jnp.where(d * each + i < slots, v, 0.0))
        o_ref[0] = jnp.concatenate(parts, axis=0).astype(BF)

    return pl.pallas_call(
        body,
        grid=(n_tp, lanes // tile),
        in_specs=[pl.BlockSpec((each, latd, tile), lambda d, l: (d, 0, l))],
        out_specs=pl.BlockSpec((1, each * latd, tile), lambda d, l: (d, 0, l)),
        out_shape=jax.ShapeDtypeStruct((n_tp, each * latd, lanes), BF),
        compiler_params=params(32),
        name="pack_rows",
    )(state)


def unpack_rows(packed, slots, latd, flat, valid, tile):
    n_tp, rows, lanes = packed.shape
    each = rows // latd
    last = lanes // tile - 1

    def body(x_ref, o_ref):
        l = pl.program_id(1)
        lane = l * tile + lax.broadcasted_iota(jnp.int32, (rows, tile), 1)
        v = jnp.where(lane < valid, x_ref[0].astype(F32), 0.0)
        for i in range(each):
            o_ref[i] = v[i * latd : (i + 1) * latd].astype(BF)

    return pl.pallas_call(
        body,
        grid=(n_tp, pl.cdiv(flat, tile)),
        in_specs=[pl.BlockSpec((1, rows, tile), lambda d, l: (d, 0, jnp.minimum(l, last)))],
        out_specs=pl.BlockSpec((each, latd, tile), lambda d, l: (d, 0, l)),
        out_shape=jax.ShapeDtypeStruct((slots, latd, flat), BF),
        compiler_params=params(32),
        name="unpack_rows",
    )(packed)


def load_transposed(x_ref, row, eye, scr, csh):
    n_tp, cv = x_ref.shape[0], x_ref.shape[2]
    for t in range(n_tp):
        scr[t * csh : t * csh + cv, :] = x_ref[t, row].astype(F32)
    return mm(eye, scr[...].astype(BF), NT)


def store_transposed(o_ref, row, value, eye, csh):
    n_tp, cv = o_ref.shape[0], o_ref.shape[2]
    vt = mm(value, eye, TN)
    for t in range(n_tp):
        o_ref[t, row] = vt[t * csh : t * csh + cv, :].astype(BF)


def fourier(grid5, fwd, eye, gain, cmask, row_mask, n_sp, each, latd, csh):
    n_tp, rows, cv, nlon = grid5.shape
    cp = n_tp * csh
    mk = fwd.shape[0] // n_sp

    def body(x_ref, fb_ref, eye_ref, g_ref, cm_ref, rm_ref, f_ref, xt_ref, scr):
        s, j = pl.program_id(0), pl.program_id(1)
        r = s * latd + j

        @pl.when(r == 0)
        def _():
            scr[...] = jnp.zeros_like(scr)

        xt = load_transposed(x_ref, 0, eye_ref[...], scr, csh) * (cm_ref[...] * rm_ref[r])
        r1 = lax.rsqrt(jnp.sum(xt * xt, axis=1, keepdims=True) / CH + EPS)
        u = (xt * r1 * g_ref[...]).astype(BF)
        f = mm(fb_ref[...], u)
        for d in range(n_sp):
            f_ref[d, 0, 0] = f[d * mk : (d + 1) * mk].astype(BF)
        xt_ref[0] = xt.astype(BF)

    return pl.pallas_call(
        body,
        grid=(each, latd),
        in_specs=[
            pl.BlockSpec((n_tp, 1, cv, nlon), lambda s, j: (0, s * latd + j, 0, 0)),
            whole(fwd.shape),
            whole(eye.shape),
            whole(gain.shape),
            whole(cmask.shape),
            SMEM,
        ],
        out_specs=[
            pl.BlockSpec((n_sp, 1, 1, mk, cp), lambda s, j: (0, j, s, 0, 0)),
            pl.BlockSpec((1, nlon, cp), lambda s, j: (s * latd + j, 0, 0)),
        ],
        out_shape=[
            jax.ShapeDtypeStruct((n_sp, latd, each, mk, cp), BF),
            jax.ShapeDtypeStruct((rows, nlon, cp), BF),
        ],
        scratch_shapes=[pltpu.VMEM((cp, nlon), F32)],
        compiler_params=params(40),
        name="fourier",
    )(grid5, fwd, eye, gain, cmask, row_mask)


def legendre(data, table, inner, per_order, name):
    n_sp, rows, cp = data.shape
    n_mi, n_out, n_in = table.shape
    out_each = n_out // n_sp
    tile = 256

    def body(x_ref, t_ref, o_ref, fin, fout):
        for d in range(n_sp):
            spread(fin, d * rows, x_ref[d])
        for i in range(inner):
            got = pick_rows(fin, i, n_in, inner)
            res = mm(t_ref[(i // per_order) % n_mi], got)
            for d in range(n_sp):
                fout[d, i * out_each : (i + 1) * out_each] = res[d * out_each : (d + 1) * out_each]
        for d in range(n_sp):
            o_ref[d] = fout[d].astype(BF)

    return pl.pallas_call(
        body,
        grid=(cp // tile,),
        in_specs=[pl.BlockSpec((n_sp, rows, tile), lambda c: (0, 0, c)), whole(table.shape)],
        out_specs=pl.BlockSpec((n_sp, inner * out_each, tile), lambda c: (0, 0, c)),
        out_shape=jax.ShapeDtypeStruct((n_sp, inner * out_each, cp), BF),
        scratch_shapes=[
            pltpu.VMEM((tile // LANE, n_sp * rows, LANE), F32),
            pltpu.VMEM((n_sp, inner * out_each, tile), F32),
        ],
        compiler_params=params(56),
        name=name,
    )(data, table)


def mix_forward(coef, weights):
    n_sp, rows, cp = coef.shape
    n_tp, own, csh, _ = weights.shape
    inner = rows // own
    count = n_sp * inner

    def body(x_ref, w_ref, o_ref, a_ref, fin):
        q = pl.program_id(0)

        @pl.when(q == 0)
        def _():
            for d in range(n_sp):
                spread(fin, d * rows, x_ref[d])

        a = pick_rows(fin, q, count, own)
        a_ref[0] = a
        b = mm(a, w_ref[...].reshape(n_tp * csh, cp), NT)
        for d in range(n_sp):
            o_ref[d, 0] = b[d * inner : (d + 1) * inner].astype(BF)

    return pl.pallas_call(
        body,
        grid=(own,),
        in_specs=[
            whole(coef.shape),
            pl.BlockSpec((n_tp, 1, csh, cp), lambda q: (0, q, 0, 0)),
        ],
        out_specs=[
            pl.BlockSpec((n_sp, 1, inner, cp), lambda q: (0, q, 0, 0)),
            pl.BlockSpec((1, count, cp), lambda q: (q, 0, 0)),
        ],
        out_shape=[
            jax.ShapeDtypeStruct((n_sp, own, inner, cp), BF),
            jax.ShapeDtypeStruct((own, count, cp), BF),
        ],
        scratch_shapes=[pltpu.VMEM((cp // LANE, n_sp * rows, LANE), F32)],
        compiler_params=params(60),
        name="mix_forward",
    )(coef, weights)


def mix_backward(grad, weights, coef):
    n_sp, rows, cp = grad.shape
    n_tp, own, csh, _ = weights.shape
    inner = rows // own
    count = n_sp * inner

    def body(x_ref, w_ref, a_ref, o_ref, g_ref, fin):
        q = pl.program_id(0)

        @pl.when(q == 0)
        def _():
            for d in range(n_sp):
                spread(fin, d * rows, x_ref[d])

        g = pick_rows(fin, q, count, own)
        da = mm(g, w_ref[...].reshape(n_tp * csh, cp))
        for d in range(n_sp):
            o_ref[d, 0] = da[d * inner : (d + 1) * inner].astype(BF)
        dw = mm(g, a_ref[0], TN)
        for t in range(n_tp):
            g_ref[t, 0] = dw[t * csh : (t + 1) * csh].astype(BF)

    return pl.pallas_call(
        body,
        grid=(own,),
        in_specs=[
            whole(grad.shape),
            pl.BlockSpec((n_tp, 1, csh, cp), lambda q: (0, q, 0, 0)),
            pl.BlockSpec((1, count, cp), lambda q: (q, 0, 0)),
        ],
        out_specs=[
            pl.BlockSpec((n_sp, 1, inner, cp), lambda q: (0, q, 0, 0)),
            pl.BlockSpec((n_tp, 1, csh, cp), lambda q: (0, q, 0, 0)),
        ],
        out_shape=[
            jax.ShapeDtypeStruct((n_sp, own, inner, cp), BF),
            jax.ShapeDtypeStruct((n_tp, own, csh, cp), BF),
        ],
        scratch_shapes=[pltpu.VMEM((cp // LANE, n_sp * rows, LANE), F32)],
        compiler_params=params(60),
        name="mix_backward",
    )(grad, weights, coef)


def row_block(latd):
    return 2 if latd % 2 == 0 else 1


def grid_block(coef, xt, cot5, w_in, w_out, inv, inv_t, eye, gain, cmask, row_mask, each, latd, csh):
    n_sp, _, rows_s, cp = coef.shape
    n_tp, rows, cv, nlon = cot5.shape
    hid = w_in.shape[0]
    mk = inv.shape[0] // n_sp
    jb = row_block(latd)
    px = jb * nlon

    def body(
        c_ref, xt_ref, ct_ref, wi_ref, wo_ref, ib_ref, it_ref, eye_ref, g_ref, cm_ref, rm_ref,
        out_ref, dg_ref, dh_ref, dwi_ref, dwo_ref, gg_ref,
        fin, scr, hs, dms,
    ):
        s, jj = pl.program_id(0), pl.program_id(1)

        @pl.when((s == 0) & (jj == 0))
        def _():
            scr[...] = jnp.zeros_like(scr)
            dwi_ref[...] = jnp.zeros_like(dwi_ref)
            dwo_ref[...] = jnp.zeros_like(dwo_ref)
            gg_ref[...] = jnp.zeros_like(gg_ref)

        @pl.when(jj == 0)
        def _():
            for d in range(n_sp):
                spread(fin, d * rows_s, c_ref[d, 0])

        for i in range(jb):
            j = jj * jb + i
            g = pick_rows(fin, j, n_sp * mk, latd)
            hs[i] = xt_ref[i].astype(F32) + mm(it_ref[...], g)
            dm = load_transposed(ct_ref, i, eye_ref[...], scr, csh)
            dms[i] = dm * (cm_ref[...] * rm_ref[s * latd + j])
        h = jnp.concatenate([hs[i] for i in range(jb)], axis=0)
        dm = jnp.concatenate([dms[i] for i in range(jb)], axis=0)
        dmb = dm.astype(BF)
        r2 = lax.rsqrt(jnp.sum(h * h, axis=1, keepdims=True) / CH + EPS)
        g1 = g_ref[...]
        v = (h * r2 * g1).astype(BF)
        z = mm(v, wi_ref[...], NT)
        t = jnp.tanh(GELU_A * (z + GELU_B * z * z * z))
        act = (0.5 * z * (1.0 + t)).astype(BF)
        slope = 0.5 * (1.0 + t) + 0.5 * z * (1.0 - t * t) * (
            GELU_A * (1.0 + 3.0 * GELU_B * z * z)
        )
        out = (h + mm(act, wo_ref[...])).astype(BF)
        dz = (slope * mm(dmb, wo_ref[...], NT)).astype(BF)
        dwo_ref[...] += mm(act, dmb, TN)
        dwi_ref[...] += mm(dz, v, TN)
        dv = mm(dz, wi_ref[...])
        gd = g1 * dv
        proj = jnp.sum(h * gd, axis=1, keepdims=True) / CH
        dh = dm + r2 * gd - h * (r2 * r2 * r2 * proj)
        gg_ref[...] += jnp.sum(dv * h * r2, axis=0, keepdims=True)
        for i in range(jb):
            part = dh[i * nlon : (i + 1) * nlon].astype(BF)
            dh_ref[i] = part
            dg = mm(ib_ref[...], part)
            for d in range(n_sp):
                dg_ref[d, i, 0] = dg[d * mk : (d + 1) * mk].astype(BF)
            store_transposed(out_ref, i, out[i * nlon : (i + 1) * nlon], eye_ref[...], csh)

    blocks = latd // jb
    rowmap = lambda s, j: (s * blocks + j, 0, 0)
    rowmap4 = lambda s, j: (0, s * blocks + j, 0, 0)
    return pl.pallas_call(
        body,
        grid=(each, blocks),
        in_specs=[
            pl.BlockSpec((n_sp, 1, rows_s, cp), lambda s, j: (0, s, 0, 0)),
            pl.BlockSpec((jb, nlon, cp), rowmap),
            pl.BlockSpec((n_tp, jb, cv, nlon), rowmap4),
            whole(w_in.shape),
            whole(w_out.shape),
            whole(inv.shape),
            whole(inv_t.shape),
            whole(eye.shape),
            whole(gain.shape),
            whole(cmask.shape),
            SMEM,
        ],
        out_specs=[
            pl.BlockSpec((n_tp, jb, cv, nlon), rowmap4),
            pl.BlockSpec((n_sp, jb, 1, mk, cp), lambda s, j: (0, j, s, 0, 0)),
            pl.BlockSpec((jb, nlon, cp), rowmap),
            pl.BlockSpec((hid, cp), lambda s, j: (0, 0)),
            pl.BlockSpec((hid, cp), lambda s, j: (0, 0)),
            pl.BlockSpec((1, cp), lambda s, j: (0, 0)),
        ],
        out_shape=[
            jax.ShapeDtypeStruct((n_tp, rows, cv, nlon), BF),
            jax.ShapeDtypeStruct((n_sp, latd, each, mk, cp), BF),
            jax.ShapeDtypeStruct((rows, nlon, cp), BF),
            jax.ShapeDtypeStruct((hid, cp), F32),
            jax.ShapeDtypeStruct((hid, cp), F32),
            jax.ShapeDtypeStruct((1, cp), F32),
        ],
        scratch_shapes=[
            pltpu.VMEM((cp // LANE, n_sp * rows_s, LANE), F32),
            pltpu.VMEM((cp, nlon), F32),
            pltpu.VMEM((jb, nlon, cp), F32),
            pltpu.VMEM((jb, nlon, cp), F32),
        ],
        compiler_params=params(62),
        name="grid_block",
    )(coef, xt, cot5, w_in, w_out, inv, inv_t, eye, gain, cmask, row_mask)


def grid_final(coef, xt, dh, fwd_t, eye, gain, cmask, row_mask, each, latd, csh, n_tp, cv):
    n_sp, _, rows_s, cp = coef.shape
    rows, nlon, _ = xt.shape
    mk2 = fwd_t.shape[1]

    def body(c_ref, xt_ref, dh_ref, ft_ref, eye_ref, g_ref, cm_ref, rm_ref, out_ref, gg_ref, fin):
        s, j = pl.program_id(0), pl.program_id(1)

        @pl.when((s == 0) & (j == 0))
        def _():
            gg_ref[...] = jnp.zeros_like(gg_ref)

        @pl.when(j == 0)
        def _():
            for d in range(n_sp):
                spread(fin, d * rows_s, c_ref[d, 0])

        g = pick_rows(fin, j, mk2, latd)
        du = mm(ft_ref[...], g)
        x = xt_ref[0].astype(F32)
        r1 = lax.rsqrt(jnp.sum(x * x, axis=1, keepdims=True) / CH + EPS)
        gd = g_ref[...] * du
        proj = jnp.sum(x * gd, axis=1, keepdims=True) / CH
        res = dh_ref[0].astype(F32) + r1 * gd - x * (r1 * r1 * r1 * proj)
        res = (res * (cm_ref[...] * rm_ref[s * latd + j])).astype(BF)
        gg_ref[...] += jnp.sum(du * x * r1, axis=0, keepdims=True)
        store_transposed(out_ref, 0, res, eye_ref[...], csh)

    rowmap = lambda s, j: (s * latd + j, 0, 0)
    return pl.pallas_call(
        body,
        grid=(each, latd),
        in_specs=[
            pl.BlockSpec((n_sp, 1, rows_s, cp), lambda s, j: (0, s, 0, 0)),
            pl.BlockSpec((1, nlon, cp), rowmap),
            pl.BlockSpec((1, nlon, cp), rowmap),
            whole(fwd_t.shape),
            whole(eye.shape),
            whole(gain.shape),
            whole(cmask.shape),
            SMEM,
        ],
        out_specs=[
            pl.BlockSpec((n_tp, 1, cv, nlon), lambda s, j: (0, s * latd + j, 0, 0)),
            pl.BlockSpec((1, cp), lambda s, j: (0, 0)),
        ],
        out_shape=[
            jax.ShapeDtypeStruct((n_tp, rows, cv, nlon), BF),
            jax.ShapeDtypeStruct((1, cp), F32),
        ],
        scratch_shapes=[pltpu.VMEM((cp // LANE, n_sp * rows_s, LANE), F32)],
        compiler_params=params(48),
        name="grid_final",
    )(coef, xt, dh, fwd_t, eye, gain, cmask, row_mask)


def adamw(param, grad, first, second, rate, decay):
    new_first = 0.5 * first + 0.5 * grad
    new_second = 0.5 * second + 0.5 * grad * grad
    update = new_first / BIAS_FIX / (jnp.sqrt(new_second / BIAS_FIX) + ADAM_EPS)
    return (param - rate * (update + decay * param), new_first, new_second)


def swap(value, axis):
    return lax.all_to_all(value, axis, split_axis=0, concat_axis=0, tiled=True)


def local(
    n_sp, n_tp,
    state, cotangent, rollout_lengths, channel_sizes, owner_slots,
    master, first_moment, second_moment, gains, gain_first, gain_second,
):
    slots, latd, flat = state.shape
    own, csh, cp = master.shape
    nlon = flat // csh
    sp, tp = lax.axis_index("sp"), lax.axis_index("tp")
    degrees = owner_slots.shape[0] - 4
    n_mi = (degrees + n_sp - 1) // n_sp
    mpad = n_mi * n_sp
    each = (slots + n_tp - 1) // n_tp
    inner = each * n_mi * 2
    nlatp = latd * n_sp
    valid = CVALID * nlon
    tile = 19 * 128
    lanes = pl.cdiv(valid, tile) * tile

    fwd, inv, analysis, synthesis = tables(NLAT, nlatp, nlon, degrees, mpad)
    fwd_t, inv_t = jnp.asarray(fwd.T), jnp.asarray(inv.T)
    fwd, inv = jnp.asarray(fwd), jnp.asarray(inv)
    eye = jnp.asarray(np.eye(nlon).astype(ml_dtypes.bfloat16))
    pick = (owner_slots[:degrees, None] == jnp.arange(n_sp * own)[None, :]).astype(BF)
    mine = lambda t: lax.dynamic_slice_in_dim(jnp.asarray(t), sp * n_mi, n_mi, 0)
    by_slot = lambda t: jnp.einsum("mlj,lq->mqj", mine(t), pick, preferred_element_type=F32).astype(BF)
    ana_q, syn_q = by_slot(analysis), by_slot(synthesis)
    ana_j, syn_j = jnp.swapaxes(ana_q, 1, 2), jnp.swapaxes(syn_q, 1, 2)

    chan = jnp.arange(cp)
    cmask = (chan % csh < channel_sizes[chan // csh]).astype(F32)
    rmask = (jnp.arange(csh) < channel_sizes[tp]).astype(F32)
    lat_mask = (sp * latd + jnp.arange(latd) < NLAT).astype(F32)
    slot_ids = tp * each + jnp.arange(each)
    live = slot_ids % ROLL < rollout_lengths[jnp.minimum(slot_ids // ROLL, rollout_lengths.shape[0] - 1)]
    live = (live & (slot_ids < slots)).astype(F32)
    row_mask = jnp.tile(lat_mask, each)
    cot_mask = (live[:, None] * lat_mask[None, :]).reshape(-1)
    cmask2 = cmask[None, :]

    copies = (master * (rmask[:, None] * cmask[None, :])[None]).astype(BF)
    hrow = (jnp.arange(2 * csh) < 2 * channel_sizes[tp]).astype(F32).reshape(2, csh)
    raw = []
    for i in range(4):
        at = owner_slots[degrees + i] - sp * own
        inside = (at >= 0) & (at < own)
        piece = lax.dynamic_index_in_dim(master, jnp.clip(at, 0, own - 1), 0, keepdims=False)
        keep = hrow[i % 2][:, None] * cmask2 * inside.astype(F32)
        raw.append((piece * keep).astype(BF))
    dense = lax.psum(jnp.stack(raw), "sp")
    gains_all = lax.all_gather(gains, "tp", axis=1, tiled=True)
    gain_a, gain_b = gains_all[:1], gains_all[1:]

    def to_grid(value):
        got = swap(pack_rows(value, n_tp, each, lanes, tile), "tp")
        return got[:, :, :valid].reshape(n_tp, each * latd, CVALID, nlon)

    def to_flat(value):
        got = value.reshape(n_tp, each * latd, valid)
        got = swap(jnp.pad(got, ((0, 0), (0, 0), (0, lanes - valid))), "tp")
        return unpack_rows(got, slots, latd, flat, valid, tile)

    x5 = to_grid(state)
    spec_w = lax.all_gather(copies, "tp", axis=0, tiled=False)
    f, xt = fourier(x5, fwd, eye, gain_a, cmask2, row_mask, n_sp, each, latd, csh)
    rows3 = lambda v: v.reshape(n_sp, -1, cp)
    f = swap(rows3(f), "sp")
    coef = swap(legendre(f, ana_q, inner, 2, "analysis"), "sp")
    cot5 = to_grid(cotangent)
    dense = lax.all_gather(dense, "tp", axis=1, tiled=False)
    w_in = dense[:2].reshape(2 * cp, cp)
    w_out = dense[2:].reshape(2 * cp, cp)
    mixed, coef_q = mix_forward(coef, spec_w)
    mixed = swap(rows3(mixed), "sp")
    synth = swap(legendre(mixed, syn_j, inner, 2, "synthesis"), "sp")
    synth = synth.reshape(n_sp, each, -1, cp)
    out5, dg, dh, dwi, dwo, gg_b = grid_block(
        synth, xt, cot5, w_in, w_out, inv, inv_t, eye, gain_b, cmask2, cot_mask, each, latd, csh
    )
    dg = swap(rows3(dg), "sp")
    result = to_flat(out5)
    db = swap(legendre(dg, syn_q, inner, 2, "synthesis_back"), "sp")
    da, dws = mix_backward(db, spec_w, coef_q)
    da = swap(rows3(da), "sp")
    df = swap(legendre(da, ana_j, inner, 2, "analysis_back"), "sp")
    df = df.reshape(n_sp, each, -1, cp)
    g5, gg_a = grid_final(
        df, xt, dh, fwd_t, eye, gain_a, cmask2, row_mask, each, latd, csh, n_tp, CVALID
    )
    grad_state = to_flat(g5)

    spec_g = lax.psum_scatter(dws, "tp", scatter_dimension=0, tiled=False).astype(F32)
    dense_g = jnp.stack([dwi, dwo]).reshape(4, n_tp, csh, cp).astype(BF)
    dense_g = lax.psum_scatter(dense_g, "tp", scatter_dimension=1, tiled=False)
    dense_g = lax.psum(dense_g.astype(F32), "sp")
    grads = spec_g
    for i in range(4):
        hit = (owner_slots[degrees + i] == sp * own + jnp.arange(own))[:, None, None]
        grads = jnp.where(hit, dense_g[i][None], grads)
    new_master, new_first, new_second = adamw(master, grads, first_moment, second_moment, 0.03, 0.01)
    gain_g = lax.psum(jnp.concatenate([gg_a, gg_b], axis=0), ("sp", "tp"))
    gain_g = lax.dynamic_slice_in_dim(gain_g, tp * csh, csh, 1)
    new_gains, gain_one, gain_two = adamw(gains, gain_g, gain_first, gain_second, 0.5, 0.0)
    return (
        result, grad_state, new_master, new_master.astype(BF), new_first, new_second,
        new_gains, gain_one, gain_two,
    )


def solution(mesh):
    wide, slot, gain = P(None, "sp", "tp"), P("sp", "tp", None), P(None, "tp")
    return jax.shard_map(
        functools.partial(local, mesh.shape["sp"], mesh.shape["tp"]),
        mesh=mesh,
        in_specs=(wide, wide, P(), P(), P(), slot, slot, slot, gain, gain, gain),
        out_specs=(wide, wide, slot, slot, slot, slot, gain, gain, gain),
        check_vma=False,
    )
```

```python
import functools
import math

import jax
import jax.numpy as jnp
import ml_dtypes
import numpy as np
from jax import lax
from jax.experimental import pallas as pl
from jax.experimental.pallas import tpu as pltpu
from jax.sharding import PartitionSpec as P

CH = 641
CVALID = 161
CROWS = 168
NLAT = 90
ROLL = 5
EPS = 1e-05
ADAM_EPS = 1e-08
BIAS_FIX = 1.0 - 0.5**5
GELU_A = math.sqrt(2.0 / math.pi)
GELU_B = 0.044715
BF = jnp.bfloat16
F32 = jnp.float32
NT = (((1,), (1,)), ((), ()))
NN = (((1,), (0,)), ((), ()))
TN = (((0,), (0,)), ((), ()))


def mm(a, b, dims=NN):
    return lax.dot_general(a, b, dims, preferred_element_type=F32)


def tables(nlat, nlatp, nlon, mmax, mpad):
    theta = (np.arange(nlat) + 0.5) * (math.pi / nlat)
    cosine, sine = np.cos(theta), np.sin(theta)
    legendre = np.zeros((mmax, mmax, nlat))
    for m in range(mmax):
        value = math.sqrt(0.5) * np.ones(nlat)
        for k in range(1, m + 1):
            value = value * math.sqrt((2 * k + 1) / (2 * k)) * sine
        legendre[m, m] = value
        if m + 1 < mmax:
            legendre[m, m + 1] = math.sqrt(2 * m + 3) * cosine * value
        for l in range(m + 2, mmax):
            a = math.sqrt((4 * l * l - 1) / (l * l - m * m))
            b = math.sqrt(((l - 1) ** 2 - m * m) / (4 * (l - 1) ** 2 - 1))
            legendre[m, l] = a * (cosine * legendre[m, l - 1] - b * legendre[m, l - 2])
    analysis = np.zeros((mpad, mmax, nlatp))
    synthesis = np.zeros((mpad, mmax, nlatp))
    analysis[:mmax, :, :nlat] = legendre * sine * (math.pi / nlat)
    synthesis[:mmax, :, :nlat] = legendre
    angle = (np.arange(mmax)[:, None] * np.arange(nlon)[None, :] % nlon) * (2.0 * math.pi / nlon)
    fwd = np.zeros((mpad, 2, nlon))
    fwd[:mmax, 0] = np.cos(angle) * math.sqrt(2.0 / nlon)
    fwd[:mmax, 1] = -np.sin(angle) * math.sqrt(2.0 / nlon)
    fwd_low = fwd.astype(np.float32).astype(ml_dtypes.bfloat16)
    inv = fwd.copy()
    inv[0] *= 0.5
    inv_low = inv.astype(np.float32).astype(ml_dtypes.bfloat16)
    low = lambda v: v.astype(np.float32).astype(ml_dtypes.bfloat16)
    return (
        fwd_low.reshape(mpad * 2, nlon),
        inv_low.reshape(mpad * 2, nlon),
        low(analysis),
        low(synthesis),
    )


def params(mib):
    return pltpu.CompilerParams(vmem_limit_bytes=mib * 2**20)


def whole(shape):
    return pl.BlockSpec(shape, lambda *_: (0,) * len(shape), pipeline_mode=pl.Buffered(1))


SMEM = pl.BlockSpec(memory_space=pltpu.SMEM)


LANE = 128


def spread(scr, start, value):
    rows, cols = value.shape
    for t in range(cols // LANE):
        scr[t, start : start + rows, :] = value[:, t * LANE : (t + 1) * LANE].astype(F32)


def pick_rows(scr, start, count, stride):
    parts = [scr[t, pl.ds(start, count, stride=stride), :] for t in range(scr.shape[0])]
    return jnp.concatenate(parts, axis=1).astype(BF)


class Plan:
    def __init__(self, slots, latd, n_sp, n_tp, n_mi):
        left = slots % n_tp
        self.split = left > 0 and latd % n_tp == 0 and n_mi % n_tp == 0
        self.slots, self.latd, self.n_tp = slots, latd, n_tp
        self.main = slots // n_tp if self.split else -(-slots // n_tp)
        self.left = left if self.split else 0
        self.part = latd // n_tp if self.split else 0
        self.chunks = [Chunk(self.main, latd, n_sp, n_mi, "sp", False)]
        if self.split:
            self.chunks.append(
                Chunk(left, self.part, n_sp * n_tp, n_mi // n_tp, ("sp", "tp"), True)
            )


class Chunk:
    def __init__(self, each, jn, nd, nm, axes, left):
        self.each, self.jn, self.nd, self.nm, self.axes, self.left = each, jn, nd, nm, axes, left
        self.rows = each * jn
        self.mk = 2 * nm
        self.inner = each * self.mk
        self.jb = 2 if jn % 2 == 0 else 1
        self.step = self.rows if left else self.jb
        self.blocks = 1 if left else jn // self.jb
        self.grid = (1, 1) if left else (each, self.blocks)
        self.stride = self.rows if left else jn

    def raw(self, i):
        return (i % self.each) * self.jn + i // self.each if self.left else i

    def row_map(self, *rest):
        return lambda s, k: (s * self.blocks + k,) + rest

    def order_spec(self, cp):
        if self.left:
            return pl.BlockSpec((self.nd, self.rows * self.mk, cp), lambda s, k: (0, 0, 0))
        return pl.BlockSpec((self.nd, self.jb, 1, self.mk, cp), lambda s, k: (0, k, s, 0, 0))

    def order_shape(self, cp):
        if self.left:
            return jax.ShapeDtypeStruct((self.nd, self.rows * self.mk, cp), BF)
        return jax.ShapeDtypeStruct((self.nd, self.jn, self.each, self.mk, cp), BF)

    def order_scratch(self, cp):
        return pltpu.VMEM((self.nd, self.step * self.mk, cp), F32)

    def keep_orders(self, fs, i, value):
        for d in range(self.nd):
            fs[d, i * self.mk : (i + 1) * self.mk] = value[d * self.mk : (d + 1) * self.mk]

    def write_orders(self, ref, fs):
        for d in range(self.nd):
            if self.left:
                ref[d] = fs[d].astype(BF)
            else:
                for i in range(self.step):
                    ref[d, i, 0] = fs[d, i * self.mk : (i + 1) * self.mk].astype(BF)

    def grid_coef(self, value):
        return value.reshape(self.nd, self.grid[0], -1, value.shape[-1])

    def coef_spec(self, rows_s, cp):
        return pl.BlockSpec((self.nd, 1, rows_s, cp), lambda s, k: (0, s, 0, 0))


def pack_rows(state, me, plan, lanes, tile):
    slots, latd, _ = state.shape
    n_tp, main, left, part = plan.n_tp, plan.main, plan.left, plan.part

    def body(me_ref, x_ref, *outs):
        for d in range(n_tp):
            t = me_ref[0] ^ d
            parts = []
            for i in range(main):
                at = t * main + i
                v = x_ref[jnp.minimum(at, slots - 1)].astype(F32)
                parts.append(jnp.where(at < slots, v, 0.0) if n_tp * main > slots else v)
            outs[d][...] = jnp.concatenate(parts, axis=0).astype(BF)
        if left:
            whole_rows = [x_ref[n_tp * main + i].astype(F32) for i in range(left)]
            options = [
                jnp.concatenate([v[t * part : (t + 1) * part] for v in whole_rows], axis=0)
                for t in range(n_tp)
            ]
            for d in range(n_tp):
                t = me_ref[0] ^ d
                acc = options[0]
                for o in range(1, n_tp):
                    acc = jnp.where(t == o, options[o], acc)
                outs[n_tp + d][...] = acc.astype(BF)

    counts = [main * latd] * n_tp + [left * part] * (n_tp if left else 0)
    got = pl.pallas_call(
        body,
        grid=(lanes // tile,),
        in_specs=[SMEM, pl.BlockSpec((slots, latd, tile), lambda l: (0, 0, l))],
        out_specs=[pl.BlockSpec((c, tile), lambda l: (0, l)) for c in counts],
        out_shape=[jax.ShapeDtypeStruct((c, lanes), BF) for c in counts],
        compiler_params=params(32),
        name="pack_rows",
    )(me, state)
    return got[:n_tp], got[n_tp:]


def unpack_rows(pieces, me, plan, flat, valid, lanes, tile):
    slots, latd, n_tp, main, left, part = (
        plan.slots, plan.latd, plan.n_tp, plan.main, plan.left, plan.part,
    )
    last = lanes // tile - 1
    arrays = [a for _, group in pieces for a in group]

    def body(me_ref, *refs):
        o_ref = refs[-1]
        lane = pl.program_id(0) * tile + lax.broadcasted_iota(jnp.int32, (1, tile), 1)
        keep = lane < valid
        for p, (first, _) in enumerate(pieces):
            group = refs[p * n_tp : (p + 1) * n_tp]
            values = [jnp.where(keep, g[...].astype(F32), 0.0) for g in group]
            if first >= 0:
                for d in range(n_tp):
                    for i in range(values[d].shape[0] // latd):
                        at = (me_ref[0] ^ d) * main + first + i

                        @pl.when(at < slots)
                        def _(at=at, d=d, i=i):
                            o_ref[at] = values[d][i * latd : (i + 1) * latd].astype(BF)
            else:
                ordered = []
                for t in range(n_tp):
                    acc = values[0]
                    for d in range(1, n_tp):
                        acc = jnp.where((me_ref[0] ^ d) == t, values[d], acc)
                    ordered.append(acc)
                for i in range(left):
                    o_ref[n_tp * main + i] = jnp.concatenate(
                        [v[i * part : (i + 1) * part] for v in ordered], axis=0
                    ).astype(BF)

    return pl.pallas_call(
        body,
        grid=(pl.cdiv(flat, tile),),
        in_specs=[SMEM]
        + [pl.BlockSpec((a.shape[0], tile), lambda l: (0, jnp.minimum(l, last))) for a in arrays],
        out_specs=pl.BlockSpec((slots, latd, tile), lambda l: (0, 0, l)),
        out_shape=jax.ShapeDtypeStruct((slots, latd, flat), BF),
        compiler_params=params(48),
        name="unpack_rows",
    )(me, *arrays)


def load_transposed(refs, row, me, eye, scr, csh):
    for d, ref in enumerate(refs):
        start = pl.multiple_of((me ^ d) * csh, 64)
        scr[pl.ds(start, ref.shape[1]), :] = ref[row].astype(F32)
    return mm(eye, scr[...].astype(BF), NT)


def store_transposed(refs, row, value, me, eye, scr, csh):
    scr[...] = mm(value, eye, TN)
    for d, ref in enumerate(refs):
        start = pl.multiple_of((me ^ d) * csh, 64)
        ref[row] = scr[pl.ds(start, ref.shape[1]), :].astype(BF)


def fourier(ck, grids, me, fwd, eye, gain, cmask, row_mask, csh):
    _, cv, nlon = grids[0].shape
    n = len(grids)
    cp = cmask.shape[1]
    step = ck.step

    def body(me_ref, fb_ref, eye_ref, g_ref, cm_ref, rm_ref, *refs):
        x_refs, (f_ref, xt_ref, scr, fs) = refs[:n], refs[n:]
        at = pl.program_id(0) * ck.blocks + pl.program_id(1)

        @pl.when(at == 0)
        def _():
            scr[...] = jnp.zeros_like(scr)

        for i in range(step):
            xt = load_transposed(x_refs, ck.raw(i), me_ref[0], eye_ref[...], scr, csh)
            xt = xt * (cm_ref[...] * rm_ref[at * step + i])
            r1 = lax.rsqrt(jnp.sum(xt * xt, axis=1, keepdims=True) / CH + EPS)
            u = (xt * r1 * g_ref[...]).astype(BF)
            ck.keep_orders(fs, i, mm(fb_ref[...], u))
            xt_ref[i] = xt.astype(BF)
        ck.write_orders(f_ref, fs)

    return pl.pallas_call(
        body,
        grid=ck.grid,
        in_specs=[SMEM]
        + [whole(fwd.shape), whole(eye.shape), whole(gain.shape), whole(cmask.shape), SMEM]
        + [pl.BlockSpec((step, cv, nlon), ck.row_map(0, 0))] * n,
        out_specs=[
            ck.order_spec(cp),
            pl.BlockSpec((step, nlon, cp), ck.row_map(0, 0)),
        ],
        out_shape=[
            ck.order_shape(cp),
            jax.ShapeDtypeStruct((ck.rows, nlon, cp), BF),
        ],
        scratch_shapes=[pltpu.VMEM((cp, nlon), F32), ck.order_scratch(cp)],
        compiler_params=params(48),
        name="fourier",
    )(me, fwd, eye, gain, cmask, row_mask, *grids)


def legendre(ck, data, table, n_dest, by_order, name):
    n_src, rows, cp = data.shape
    n_mi, n_out, n_in = table.shape
    inner = ck.inner
    out_each = n_out // n_dest
    tile = 256

    def body(x_ref, t_ref, o_ref, fin, fout):
        for d in range(n_src):
            spread(fin, d * rows, x_ref[d])
        for i in range(inner):
            got = pick_rows(fin, i, n_in, inner)
            res = mm(t_ref[(i // 2) % n_mi], got)
            at = i % ck.mk * ck.each + i // ck.mk if by_order and ck.left else i
            for d in range(n_dest):
                fout[d, at * out_each : (at + 1) * out_each] = res[d * out_each : (d + 1) * out_each]
        for d in range(n_dest):
            o_ref[d] = fout[d].astype(BF)

    return pl.pallas_call(
        body,
        grid=(cp // tile,),
        in_specs=[pl.BlockSpec((n_src, rows, tile), lambda c: (0, 0, c)), whole(table.shape)],
        out_specs=pl.BlockSpec((n_dest, inner * out_each, tile), lambda c: (0, 0, c)),
        out_shape=jax.ShapeDtypeStruct((n_dest, inner * out_each, cp), BF),
        scratch_shapes=[
            pltpu.VMEM((tile // LANE, n_src * rows, LANE), F32),
            pltpu.VMEM((n_dest, inner * out_each, tile), F32),
        ],
        compiler_params=params(56),
        name=name,
    )(data, table)


def mix(ck, coef, weights, csh, dims, name):
    n_sp, rows, cp = coef.shape
    n_tp, own, wrows, _ = weights.shape
    inner = ck.inner
    count = n_sp * inner
    qb = next((b for b in range(1, own + 1) if own % b == 0 and b * inner % 16 == 0), own)

    def body(x_ref, w_ref, o_ref, a_ref, fin, fout, wfull):
        k = pl.program_id(0)

        @pl.when(k == 0)
        def _():
            wfull[...] = jnp.zeros_like(wfull)
            for d in range(n_sp):
                spread(fin, d * rows, x_ref[d])

        for i in range(qb):
            a = pick_rows(fin, k * qb + i, count, own)
            a_ref[i] = a
            for t in range(n_tp):
                wfull[t * csh : t * csh + wrows] = w_ref[t, i]
            b = mm(a, wfull[...], dims)
            for d in range(n_sp):
                fout[d, i * inner : (i + 1) * inner] = b[d * inner : (d + 1) * inner]
        for d in range(n_sp):
            o_ref[d] = fout[d].astype(BF)

    return pl.pallas_call(
        body,
        grid=(own // qb,),
        in_specs=[
            whole(coef.shape),
            pl.BlockSpec((n_tp, qb, wrows, cp), lambda k: (0, k, 0, 0)),
        ],
        out_specs=[
            pl.BlockSpec((n_sp, qb * inner, cp), lambda k: (0, k, 0)),
            pl.BlockSpec((qb, count, cp), lambda k: (k, 0, 0)),
        ],
        out_shape=[
            jax.ShapeDtypeStruct((n_sp, own * inner, cp), BF),
            jax.ShapeDtypeStruct((own, count, cp), BF),
        ],
        scratch_shapes=[
            pltpu.VMEM((cp // LANE, n_sp * rows, LANE), F32),
            pltpu.VMEM((n_sp, qb * inner, cp), F32),
            pltpu.VMEM((n_tp * csh, cp), BF),
        ],
        compiler_params=params(56),
        name=name,
    )(coef, weights)


def weight_grads(grads, coefs, n_tp, wrows):
    n = len(grads)
    own, _, cp = grads[0].shape
    csh = cp // n_tp

    def body(*refs):
        o_ref = refs[-1]
        g = jnp.concatenate([r[0] for r in refs[:n]], axis=0)
        a = jnp.concatenate([r[0] for r in refs[n : 2 * n]], axis=0)
        dw = mm(g, a, TN)
        for t in range(n_tp):
            o_ref[t, 0] = dw[t * csh : t * csh + wrows].astype(BF)

    return pl.pallas_call(
        body,
        grid=(own,),
        in_specs=[pl.BlockSpec((1,) + v.shape[1:], lambda q: (q, 0, 0)) for v in grads + coefs],
        out_specs=pl.BlockSpec((n_tp, 1, wrows, cp), lambda q: (0, q, 0, 0)),
        out_shape=jax.ShapeDtypeStruct((n_tp, own, wrows, cp), BF),
        compiler_params=params(48),
        name="weight_grads",
    )(*grads, *coefs)


def grid_block(ck, coef, xt, cots, me, w_in, w_out, inv, inv_t, eye, gain, cmask, row_mask, csh):
    nd, _, rows_s, cp = coef.shape
    _, cv, nlon = cots[0].shape
    n = len(cots)
    hid = w_in.shape[0]
    rows, step, mk = ck.rows, ck.step, ck.mk
    jb = 2 if step % 2 == 0 else 1

    def body(me_ref, c_ref, xt_ref, wi_ref, wo_ref, ib_ref, it_ref, eye_ref, g_ref, cm_ref, rm_ref, *refs):
        ct_refs, out_refs = refs[:n], refs[n : 2 * n]
        dg_ref, dh_ref, dwi_ref, dwo_ref, gg_ref, fin, scr, oscr, hs, dms, fs = refs[2 * n :]
        k = pl.program_id(1)
        at = pl.program_id(0) * ck.blocks + k

        @pl.when(at == 0)
        def _():
            scr[...] = jnp.zeros_like(scr)
            dwi_ref[...] = jnp.zeros_like(dwi_ref)
            dwo_ref[...] = jnp.zeros_like(dwo_ref)
            gg_ref[...] = jnp.zeros_like(gg_ref)

        @pl.when(k == 0)
        def _():
            for d in range(nd):
                spread(fin, d * rows_s, c_ref[d, 0])

        for base in range(0, step, jb):
            for i in range(jb):
                r = base + i
                g = pick_rows(fin, k * ck.jb + ck.raw(r), nd * mk, ck.stride)
                hs[i] = xt_ref[r].astype(F32) + mm(it_ref[...], g)
                dm = load_transposed(ct_refs, ck.raw(r), me_ref[0], eye_ref[...], scr, csh)
                dms[i] = dm * (cm_ref[...] * rm_ref[at * step + r])
            h = jnp.concatenate([hs[i] for i in range(jb)], axis=0)
            dm = jnp.concatenate([dms[i] for i in range(jb)], axis=0)
            dmb = dm.astype(BF)
            r2 = lax.rsqrt(jnp.sum(h * h, axis=1, keepdims=True) / CH + EPS)
            g1 = g_ref[...]
            v = (h * r2 * g1).astype(BF)
            z = mm(v, wi_ref[...], NT)
            t = jnp.tanh(GELU_A * (z + GELU_B * z * z * z))
            act = (0.5 * z * (1.0 + t)).astype(BF)
            slope = 0.5 * (1.0 + t) + 0.5 * z * (1.0 - t * t) * (
                GELU_A * (1.0 + 3.0 * GELU_B * z * z)
            )
            out = (h + mm(act, wo_ref[...])).astype(BF)
            dz = (slope * mm(dmb, wo_ref[...], NT)).astype(BF)
            dwo_ref[...] += mm(act, dmb, TN)
            dwi_ref[...] += mm(dz, v, TN)
            dv = mm(dz, wi_ref[...])
            gd = g1 * dv
            proj = jnp.sum(h * gd, axis=1, keepdims=True) / CH
            dh = dm + r2 * gd - h * (r2 * r2 * r2 * proj)
            gg_ref[...] += jnp.sum(dv * h * r2, axis=0, keepdims=True)
            for i in range(jb):
                r = base + i
                part = dh[i * nlon : (i + 1) * nlon].astype(BF)
                dh_ref[r] = part
                ck.keep_orders(fs, r, mm(ib_ref[...], part))
                store_transposed(
                    out_refs, ck.raw(r), out[i * nlon : (i + 1) * nlon], me_ref[0], eye_ref[...], oscr, csh
                )
        ck.write_orders(dg_ref, fs)

    rowmap = ck.row_map(0, 0)
    fixed = lambda s, k: (0, 0)
    grid_spec = pl.BlockSpec((step, cv, nlon), rowmap)
    got = pl.pallas_call(
        body,
        grid=ck.grid,
        in_specs=[
            SMEM,
            ck.coef_spec(rows_s, cp),
            pl.BlockSpec((step, nlon, cp), rowmap),
            whole(w_in.shape),
            whole(w_out.shape),
            whole(inv.shape),
            whole(inv_t.shape),
            whole(eye.shape),
            whole(gain.shape),
            whole(cmask.shape),
            SMEM,
        ]
        + [grid_spec] * n,
        out_specs=[grid_spec] * n
        + [
            ck.order_spec(cp),
            pl.BlockSpec((step, nlon, cp), rowmap),
            pl.BlockSpec((hid, cp), fixed),
            pl.BlockSpec((hid, cp), fixed),
            pl.BlockSpec((1, cp), fixed),
        ],
        out_shape=[jax.ShapeDtypeStruct((rows, cv, nlon), BF)] * n
        + [
            ck.order_shape(cp),
            jax.ShapeDtypeStruct((rows, nlon, cp), BF),
            jax.ShapeDtypeStruct((hid, cp), F32),
            jax.ShapeDtypeStruct((hid, cp), F32),
            jax.ShapeDtypeStruct((1, cp), F32),
        ],
        scratch_shapes=[
            pltpu.VMEM((cp // LANE, nd * rows_s, LANE), F32),
            pltpu.VMEM((cp, nlon), F32),
            pltpu.VMEM((cp, nlon), F32),
            pltpu.VMEM((jb, nlon, cp), F32),
            pltpu.VMEM((jb, nlon, cp), F32),
            ck.order_scratch(cp),
        ],
        compiler_params=params(62),
        name="grid_block",
    )(me, coef, xt, w_in, w_out, inv, inv_t, eye, gain, cmask, row_mask, *cots)
    return got[:n], got[n:]


def grid_final(ck, coef, xt, dh, me, fwd_t, eye, gain, cmask, row_mask, csh, n, cv):
    nd, _, rows_s, cp = coef.shape
    rows, nlon, _ = xt.shape
    step, mk = ck.step, ck.mk

    def body(me_ref, c_ref, xt_ref, dh_ref, ft_ref, eye_ref, g_ref, cm_ref, rm_ref, *refs):
        out_refs, (gg_ref, fin, oscr) = refs[:n], refs[n:]
        k = pl.program_id(1)
        at = pl.program_id(0) * ck.blocks + k

        @pl.when(at == 0)
        def _():
            gg_ref[...] = jnp.zeros_like(gg_ref)

        @pl.when(k == 0)
        def _():
            for d in range(nd):
                spread(fin, d * rows_s, c_ref[d, 0])

        for i in range(step):
            du = mm(ft_ref[...], pick_rows(fin, k * ck.jb + ck.raw(i), nd * mk, ck.stride))
            x = xt_ref[i].astype(F32)
            r1 = lax.rsqrt(jnp.sum(x * x, axis=1, keepdims=True) / CH + EPS)
            gd = g_ref[...] * du
            proj = jnp.sum(x * gd, axis=1, keepdims=True) / CH
            res = dh_ref[i].astype(F32) + r1 * gd - x * (r1 * r1 * r1 * proj)
            res = (res * (cm_ref[...] * rm_ref[at * step + i])).astype(BF)
            gg_ref[...] += jnp.sum(du * x * r1, axis=0, keepdims=True)
            store_transposed(out_refs, ck.raw(i), res, me_ref[0], eye_ref[...], oscr, csh)

    rowmap = ck.row_map(0, 0)
    got = pl.pallas_call(
        body,
        grid=ck.grid,
        in_specs=[
            SMEM,
            ck.coef_spec(rows_s, cp),
            pl.BlockSpec((step, nlon, cp), rowmap),
            pl.BlockSpec((step, nlon, cp), rowmap),
            whole(fwd_t.shape),
            whole(eye.shape),
            whole(gain.shape),
            whole(cmask.shape),
            SMEM,
        ],
        out_specs=[pl.BlockSpec((step, cv, nlon), rowmap)] * n
        + [pl.BlockSpec((1, cp), lambda s, k: (0, 0))],
        out_shape=[jax.ShapeDtypeStruct((rows, cv, nlon), BF)] * n
        + [jax.ShapeDtypeStruct((1, cp), F32)],
        scratch_shapes=[
            pltpu.VMEM((cp // LANE, nd * rows_s, LANE), F32),
            pltpu.VMEM((cp, nlon), F32),
        ],
        compiler_params=params(48),
        name="grid_final",
    )(me, coef, xt, dh, fwd_t, eye, gain, cmask, row_mask)
    return got[:n], got[n]


def adamw(param, grad, first, second, rate, decay):
    new_first = 0.5 * first + 0.5 * grad
    new_second = 0.5 * second + 0.5 * grad * grad
    update = new_first / BIAS_FIX / (jnp.sqrt(new_second / BIAS_FIX) + ADAM_EPS)
    return (param - rate * (update + decay * param), new_first, new_second)


def swap(value, axis):
    return lax.all_to_all(value, axis, split_axis=0, concat_axis=0, tiled=True)


def after(value, *others):
    return lax.optimization_barrier((value, others))[0]


def local(
    n_sp, n_tp,
    state, cotangent, rollout_lengths, channel_sizes, owner_slots,
    master, first_moment, second_moment, gains, gain_first, gain_second,
):
    slots, latd, flat = state.shape
    own, csh, cp = master.shape
    nlon = flat // csh
    sp, tp = lax.axis_index("sp"), lax.axis_index("tp")
    me = tp.astype(jnp.int32).reshape(1)
    degrees = owner_slots.shape[0] - 4
    n_mi = (degrees + n_sp - 1) // n_sp
    mpad = n_mi * n_sp
    plan = Plan(slots, latd, n_sp, n_tp, n_mi)
    chunks = plan.chunks
    nlatp = latd * n_sp
    valid = CVALID * nlon
    tile = 19 * 128
    lanes = pl.cdiv(valid, tile) * tile

    fwd, inv, analysis, synthesis = tables(NLAT, nlatp, nlon, degrees, mpad)
    fwd_t, inv_t = jnp.asarray(fwd.T), jnp.asarray(inv.T)
    fwd, inv = jnp.asarray(fwd), jnp.asarray(inv)
    eye = jnp.asarray(np.eye(nlon).astype(ml_dtypes.bfloat16))
    pick = (owner_slots[:degrees, None] == jnp.arange(n_sp * own)[None, :]).astype(BF)
    mine = lambda t: lax.dynamic_slice_in_dim(jnp.asarray(t), sp * n_mi, n_mi, 0)
    by_slot = lambda t: jnp.einsum("mlj,lq->mqj", mine(t), pick, preferred_element_type=F32).astype(BF)
    ana_q, syn_q = by_slot(analysis), by_slot(synthesis)
    ana_j, syn_j = jnp.swapaxes(ana_q, 1, 2), jnp.swapaxes(syn_q, 1, 2)

    def table(ck, t):
        return t if ck.nm == n_mi else lax.dynamic_slice_in_dim(t, tp * ck.nm, ck.nm, 0)

    chan = jnp.arange(cp)
    cmask = (chan % csh < channel_sizes[chan // csh]).astype(F32)
    rmask = (jnp.arange(csh) < channel_sizes[tp]).astype(F32)
    cmask2 = cmask[None, :]
    samples = rollout_lengths.shape[0]
    row_masks, cot_masks = [], []
    for ck in chunks:
        first, lat0 = (n_tp * plan.main, tp * ck.jn) if ck.left else (tp * plan.main, 0)
        ids = first + jnp.arange(ck.each)
        live = ids % ROLL < rollout_lengths[jnp.minimum(ids // ROLL, samples - 1)]
        live = (live & (ids < slots)).astype(F32)
        lat = (sp * latd + lat0 + jnp.arange(ck.jn) < NLAT).astype(F32)
        masks = jnp.ones((ck.each, 1), F32) * lat[None, :], live[:, None] * lat[None, :]
        masks = [(m.T if ck.left else m).reshape(-1) for m in masks]
        row_masks.append(masks[0])
        cot_masks.append(masks[1])

    copies = (master * (rmask[:, None] * cmask2)[None]).astype(BF)
    hrow = (jnp.arange(2 * csh) < 2 * channel_sizes[tp]).astype(F32).reshape(2, csh)
    raw = []
    for i in range(4):
        at = owner_slots[degrees + i] - sp * own
        inside = (at >= 0) & (at < own)
        piece = lax.dynamic_index_in_dim(master, jnp.clip(at, 0, own - 1), 0, keepdims=False)
        keep = hrow[i % 2][:, None] * cmask2 * inside.astype(F32)
        raw.append((piece * keep).astype(BF))
    gains_all = swap(jnp.broadcast_to(gains[None], (n_tp,) + gains.shape), "tp")
    gains_all = jnp.swapaxes(gains_all, 0, 1).reshape(2, cp)

    cut = lambda a: a[:, :valid].reshape(-1, CVALID, nlon)
    flat_of = lambda a: jnp.pad(a.reshape(a.shape[0], valid), ((0, 0), (0, lanes - valid)))
    send = lambda a, d: lax.ppermute(a, "tp", [(i, i ^ d) for i in range(n_tp)]) if d else a
    send_all = lambda arrays: [send(a, d) for d, a in enumerate(arrays)]
    rows3 = lambda v: v.reshape(v.shape[0], -1, cp)

    main, left = pack_rows(state, me, plan, lanes, tile)
    dense = lax.psum_scatter(jnp.stack(raw), "sp", scatter_dimension=1, tiled=True)
    main, left = send_all(main), send_all(left)
    dense = lax.all_gather(after(dense, main[1]), ("tp", "sp"), axis=1, tiled=True)
    w_in = dense[:2].reshape(2 * cp, cp)
    w_out = dense[2:].reshape(2 * cp, cp)
    main, left = [cut(a) for a in main], [cut(a) for a in left]
    x5 = [main, left]
    spec_w = lax.all_gather(after(copies[:, :CROWS], main, left), "tp", axis=0, tiled=False)
    gain_a, gain_b = gains_all[:1], gains_all[1:]
    n = len(chunks)
    odd = lambda arrays: [send(a, d) if d % 2 else a for d, a in enumerate(arrays)]
    even = lambda arrays: [a if d % 2 else send(a, d) for d, a in enumerate(arrays)]

    coefs, xts = [], []
    for i, ck in enumerate(chunks):
        f, xt = fourier(ck, x5[i], me, fwd, eye, gain_a, cmask2, row_masks[i], csh)
        xts.append(xt)
        f = swap(rows3(f), ck.axes)
        c = legendre(ck, f, table(ck, ana_q), n_sp, False, "analysis")
        coefs.append(swap(c, "sp"))
    m, a = mix(chunks[0], after(coefs[0], dense), spec_w, csh, NT, "mix_forward")
    mixed, coef_q = [swap(m, "sp")], [a]
    main, left = pack_rows(after(cotangent, m), me, plan, lanes, tile)
    ahead = odd(main)
    if n > 1:
        m, a = mix(chunks[1], after(coefs[1], main), spec_w, csh, NT, "mix_forward")
        mixed.append(swap(after(m, ahead), "sp"))
        coef_q.append(a)
    main, left = after((ahead, left), mixed[0])
    main, left = even(main), send_all(left)
    synth = [
        legendre(ck, m, table(ck, syn_j), ck.nd, True, "synthesis") for ck, m in zip(chunks, mixed)
    ]
    if n > 1:
        synth[1] = after(synth[1], main, left)
    synth = [ck.grid_coef(swap(g, ck.axes)) for ck, g in zip(chunks, synth)]
    cot5 = [[cut(a) for a in main], [cut(a) for a in left]]
    outs, rest, dgs = [], [], []
    for i, ck in enumerate(chunks):
        o, r = grid_block(
            ck, synth[i], xts[i], cot5[i], me, w_in, w_out, inv, inv_t, eye, gain_b, cmask2,
            cot_masks[i], csh,
        )
        outs.append([flat_of(a) for a in o])
        rest.append(r)
        dgs.append(rows3(r[0]))
    main, left = odd(outs[0]), outs[1] if n > 1 else []
    if n > 1:
        dgs[1] = after(dgs[1], main)
    dgs = [swap(g, ck.axes) for ck, g in zip(chunks, dgs)]
    main, left = after((main, left), dgs[0])
    main, left = even(main), send_all(left)
    dbs = [
        legendre(ck, g, table(ck, syn_q), n_sp, False, "synthesis_back")
        for ck, g in zip(chunks, dgs)
    ]
    if n > 1:
        dbs[1] = after(dbs[1], main, left)
    dbs = [swap(b, "sp") for b in dbs]
    das = [mix(ck, b, spec_w, csh, NN, "mix_backward") for ck, b in zip(chunks, dbs)]
    grad_q = [a[1] for a in das]
    das = [swap(a[0], "sp") for a in das]
    pieces_out = [(0, main)] + ([(-1, left)] if left else [])
    result = unpack_rows(pieces_out, me, plan, flat, valid, lanes, tile)
    dws = weight_grads(grad_q, coef_q, n_tp, CROWS)
    dfs = [
        legendre(ck, a, table(ck, ana_j), ck.nd, True, "analysis_back") for ck, a in zip(chunks, das)
    ]
    dfs[0] = swap(dfs[0], chunks[0].axes)
    if n > 1:
        dfs[1] = swap(after(dfs[1], dfs[0]), chunks[1].axes)
    pieces, gg_a = [], 0.0
    for i, ck in enumerate(chunks):
        o, gg = grid_final(
            ck, ck.grid_coef(dfs[i]), xts[i], rest[i][1], me, fwd_t, eye, gain_a, cmask2,
            row_masks[i], csh, n_tp, CVALID,
        )
        gg_a = gg_a + gg
        pieces.append((-1 if ck.left else 0, send_all([flat_of(a) for a in o])))

    dwi = sum(r[2] for r in rest)
    dwo = sum(r[3] for r in rest)
    gg_b = sum(r[4] for r in rest)
    dense_g = jnp.stack([dwi, dwo]).reshape(4, n_tp, csh, cp).astype(BF)
    dense_g = lax.psum_scatter(after(dense_g, pieces_out), "tp", scatter_dimension=1, tiled=False)
    spec_g = lax.psum_scatter(after(dws, pieces_out), "tp", scatter_dimension=0, tiled=False)
    dense_g = lax.psum(dense_g.astype(F32), "sp")
    spec_g = jnp.pad(spec_g.astype(F32), ((0, 0), (0, csh - CROWS), (0, 0)))
    grads = spec_g
    for i in range(4):
        hit = (owner_slots[degrees + i] == sp * own + jnp.arange(own))[:, None, None]
        grads = jnp.where(hit, dense_g[i][None], grads)
    new_master, new_first, new_second = adamw(master, grads, first_moment, second_moment, 0.03, 0.01)
    gain_g = lax.psum(after(jnp.concatenate([gg_a, gg_b], axis=0), new_master), ("sp", "tp"))
    gain_g = lax.dynamic_slice_in_dim(gain_g, tp * csh, csh, 1)
    new_gains, gain_one, gain_two = adamw(gains, gain_g, gain_first, gain_second, 0.5, 0.0)
    grad_state = unpack_rows(
        pieces, after(me, new_gains, new_master), plan, flat, valid, lanes, tile
    )
    return (
        result, grad_state, new_master, new_master.astype(BF), new_first, new_second,
        new_gains, gain_one, gain_two,
    )


def solution(mesh):
    wide, slot, gain = P(None, "sp", "tp"), P("sp", "tp", None), P(None, "tp")
    return jax.shard_map(
        functools.partial(local, mesh.shape["sp"], mesh.shape["tp"]),
        mesh=mesh,
        in_specs=(wide, wide, P(), P(), P(), slot, slot, slot, gain, gain, gain),
        out_specs=(wide, wide, slot, slot, slot, slot, gain, gain, gain),
        check_vma=False,
    )
```

```python
import functools
import math

import jax
import jax.numpy as jnp
import ml_dtypes
import numpy as np
from jax import lax
from jax.experimental import pallas as pl
from jax.experimental.pallas import tpu as pltpu
from jax.sharding import PartitionSpec as P

CH = 641
CVALID = 161
CROWS = 168
NLAT = 90
ROLL = 5
EPS = 1e-05
ADAM_EPS = 1e-08
BIAS_FIX = 1.0 - 0.5**5
GELU_A = math.sqrt(2.0 / math.pi)
GELU_B = 0.044715
BF = jnp.bfloat16
F32 = jnp.float32
NT = (((1,), (1,)), ((), ()))
NN = (((1,), (0,)), ((), ()))
TN = (((0,), (0,)), ((), ()))


def mm(a, b, dims=NN):
    return lax.dot_general(a, b, dims, preferred_element_type=F32)


def tables(nlat, nlatp, nlon, mmax, mpad):
    theta = (np.arange(nlat) + 0.5) * (math.pi / nlat)
    cosine, sine = np.cos(theta), np.sin(theta)
    legendre = np.zeros((mmax, mmax, nlat))
    for m in range(mmax):
        value = math.sqrt(0.5) * np.ones(nlat)
        for k in range(1, m + 1):
            value = value * math.sqrt((2 * k + 1) / (2 * k)) * sine
        legendre[m, m] = value
        if m + 1 < mmax:
            legendre[m, m + 1] = math.sqrt(2 * m + 3) * cosine * value
        for l in range(m + 2, mmax):
            a = math.sqrt((4 * l * l - 1) / (l * l - m * m))
            b = math.sqrt(((l - 1) ** 2 - m * m) / (4 * (l - 1) ** 2 - 1))
            legendre[m, l] = a * (cosine * legendre[m, l - 1] - b * legendre[m, l - 2])
    analysis = np.zeros((mpad, mmax, nlatp))
    synthesis = np.zeros((mpad, mmax, nlatp))
    analysis[:mmax, :, :nlat] = legendre * sine * (math.pi / nlat)
    synthesis[:mmax, :, :nlat] = legendre
    angle = (np.arange(mmax)[:, None] * np.arange(nlon)[None, :] % nlon) * (2.0 * math.pi / nlon)
    fwd = np.zeros((mpad, 2, nlon))
    fwd[:mmax, 0] = np.cos(angle) * math.sqrt(2.0 / nlon)
    fwd[:mmax, 1] = -np.sin(angle) * math.sqrt(2.0 / nlon)
    fwd_low = fwd.astype(np.float32).astype(ml_dtypes.bfloat16)
    inv = fwd.copy()
    inv[0] *= 0.5
    inv_low = inv.astype(np.float32).astype(ml_dtypes.bfloat16)
    low = lambda v: v.astype(np.float32).astype(ml_dtypes.bfloat16)
    return (
        fwd_low.reshape(mpad * 2, nlon),
        inv_low.reshape(mpad * 2, nlon),
        low(analysis),
        low(synthesis),
    )


def params(mib):
    return pltpu.CompilerParams(vmem_limit_bytes=mib * 2**20)


def whole(shape):
    return pl.BlockSpec(shape, lambda *_: (0,) * len(shape), pipeline_mode=pl.Buffered(1))


SMEM = pl.BlockSpec(memory_space=pltpu.SMEM)


LANE = 128


def spread(scr, start, value):
    rows, cols = value.shape
    for t in range(cols // LANE):
        scr[t, start : start + rows, :] = value[:, t * LANE : (t + 1) * LANE].astype(F32)


def pick_rows(scr, start, count, stride):
    parts = [scr[t, pl.ds(start, count, stride=stride), :] for t in range(scr.shape[0])]
    return jnp.concatenate(parts, axis=1).astype(BF)


class Plan:
    def __init__(self, slots, latd, n_sp, n_tp, n_mi):
        left = slots % n_tp
        self.split = left > 0 and latd % n_tp == 0 and n_mi % n_tp == 0
        self.slots, self.latd, self.n_tp = slots, latd, n_tp
        self.main = slots // n_tp if self.split else -(-slots // n_tp)
        self.left = left if self.split else 0
        self.part = latd // n_tp if self.split else 0
        self.chunks = [Chunk(self.main, latd, n_sp, n_mi, "sp", False)]
        if self.split:
            self.chunks.append(
                Chunk(left, self.part, n_sp * n_tp, n_mi // n_tp, ("sp", "tp"), True)
            )


class Chunk:
    def __init__(self, each, jn, nd, nm, axes, left):
        self.each, self.jn, self.nd, self.nm, self.axes, self.left = each, jn, nd, nm, axes, left
        self.rows = each * jn
        self.mk = 2 * nm
        self.inner = each * self.mk
        self.jb = 2 if jn % 2 == 0 else 1
        self.step = self.rows if left else self.jb
        self.blocks = 1 if left else jn // self.jb
        self.grid = (1, 1) if left else (each, self.blocks)
        self.stride = self.rows if left else jn

    def raw(self, i):
        return (i % self.each) * self.jn + i // self.each if self.left else i

    def row_map(self, *rest):
        return lambda s, k: (s * self.blocks + k,) + rest

    def order_spec(self, cp):
        if self.left:
            return pl.BlockSpec((self.nd, self.rows * self.mk, cp), lambda s, k: (0, 0, 0))
        return pl.BlockSpec((self.nd, self.jb, 1, self.mk, cp), lambda s, k: (0, k, s, 0, 0))

    def order_shape(self, cp):
        if self.left:
            return jax.ShapeDtypeStruct((self.nd, self.rows * self.mk, cp), BF)
        return jax.ShapeDtypeStruct((self.nd, self.jn, self.each, self.mk, cp), BF)

    def order_scratch(self, cp):
        return pltpu.VMEM((self.nd, self.step * self.mk, cp), F32)

    def keep_orders(self, fs, i, value):
        for d in range(self.nd):
            fs[d, i * self.mk : (i + 1) * self.mk] = value[d * self.mk : (d + 1) * self.mk]

    def write_orders(self, ref, fs):
        for d in range(self.nd):
            if self.left:
                ref[d] = fs[d].astype(BF)
            else:
                for i in range(self.step):
                    ref[d, i, 0] = fs[d, i * self.mk : (i + 1) * self.mk].astype(BF)

    def grid_coef(self, value):
        return value.reshape(self.nd, self.grid[0], -1, value.shape[-1])

    def coef_spec(self, rows_s, cp):
        return pl.BlockSpec((self.nd, 1, rows_s, cp), lambda s, k: (0, s, 0, 0))


def pack_rows(state, me, plan, lanes, tile):
    slots, latd, _ = state.shape
    n_tp, main, left, part = plan.n_tp, plan.main, plan.left, plan.part

    def body(me_ref, x_ref, *outs):
        for d in range(n_tp):
            t = me_ref[0] ^ d
            parts = []
            for i in range(main):
                at = t * main + i
                v = x_ref[jnp.minimum(at, slots - 1)].astype(F32)
                parts.append(jnp.where(at < slots, v, 0.0) if n_tp * main > slots else v)
            outs[d][...] = jnp.concatenate(parts, axis=0).astype(BF)
        if left:
            whole_rows = [x_ref[n_tp * main + i].astype(F32) for i in range(left)]
            options = [
                jnp.concatenate([v[t * part : (t + 1) * part] for v in whole_rows], axis=0)
                for t in range(n_tp)
            ]
            for d in range(n_tp):
                t = me_ref[0] ^ d
                acc = options[0]
                for o in range(1, n_tp):
                    acc = jnp.where(t == o, options[o], acc)
                outs[n_tp + d][...] = acc.astype(BF)

    counts = [main * latd] * n_tp + [left * part] * (n_tp if left else 0)
    got = pl.pallas_call(
        body,
        grid=(lanes // tile,),
        in_specs=[SMEM, pl.BlockSpec((slots, latd, tile), lambda l: (0, 0, l))],
        out_specs=[pl.BlockSpec((c, tile), lambda l: (0, l)) for c in counts],
        out_shape=[jax.ShapeDtypeStruct((c, lanes), BF) for c in counts],
        compiler_params=params(32),
        name="pack_rows",
    )(me, state)
    return got[:n_tp], got[n_tp:]


def unpack_rows(pieces, me, plan, flat, valid, lanes, tile):
    slots, latd, n_tp, main, left, part = (
        plan.slots, plan.latd, plan.n_tp, plan.main, plan.left, plan.part,
    )
    last = lanes // tile - 1
    arrays = [a for _, group in pieces for a in group]

    def body(me_ref, *refs):
        o_ref = refs[-1]
        lane = pl.program_id(0) * tile + lax.broadcasted_iota(jnp.int32, (1, tile), 1)
        keep = lane < valid
        for p, (first, _) in enumerate(pieces):
            group = refs[p * n_tp : (p + 1) * n_tp]
            values = [jnp.where(keep, g[...].astype(F32), 0.0) for g in group]
            if first >= 0:
                for d in range(n_tp):
                    for i in range(values[d].shape[0] // latd):
                        at = (me_ref[0] ^ d) * main + first + i

                        @pl.when(at < slots)
                        def _(at=at, d=d, i=i):
                            o_ref[at] = values[d][i * latd : (i + 1) * latd].astype(BF)
            else:
                ordered = []
                for t in range(n_tp):
                    acc = values[0]
                    for d in range(1, n_tp):
                        acc = jnp.where((me_ref[0] ^ d) == t, values[d], acc)
                    ordered.append(acc)
                for i in range(left):
                    o_ref[n_tp * main + i] = jnp.concatenate(
                        [v[i * part : (i + 1) * part] for v in ordered], axis=0
                    ).astype(BF)

    return pl.pallas_call(
        body,
        grid=(pl.cdiv(flat, tile),),
        in_specs=[SMEM]
        + [pl.BlockSpec((a.shape[0], tile), lambda l: (0, jnp.minimum(l, last))) for a in arrays],
        out_specs=pl.BlockSpec((slots, latd, tile), lambda l: (0, 0, l)),
        out_shape=jax.ShapeDtypeStruct((slots, latd, flat), BF),
        compiler_params=params(48),
        name="unpack_rows",
    )(me, *arrays)


def load_transposed(refs, row, me, eye, scr, csh):
    for d, ref in enumerate(refs):
        start = pl.multiple_of((me ^ d) * csh, 64)
        scr[pl.ds(start, ref.shape[1]), :] = ref[row].astype(F32)
    return mm(eye, scr[...].astype(BF), NT)


def store_transposed(refs, row, value, me, eye, scr, csh):
    scr[...] = mm(value, eye, TN)
    for d, ref in enumerate(refs):
        start = pl.multiple_of((me ^ d) * csh, 64)
        ref[row] = scr[pl.ds(start, ref.shape[1]), :].astype(BF)


def fourier(ck, grids, me, fwd, eye, gain, cmask, row_mask, csh):
    _, cv, nlon = grids[0].shape
    n = len(grids)
    cp = cmask.shape[1]
    step = ck.step

    def body(me_ref, fb_ref, eye_ref, g_ref, cm_ref, rm_ref, *refs):
        x_refs, (f_ref, xt_ref, scr, fs) = refs[:n], refs[n:]
        at = pl.program_id(0) * ck.blocks + pl.program_id(1)

        @pl.when(at == 0)
        def _():
            scr[...] = jnp.zeros_like(scr)

        for i in range(step):
            xt = load_transposed(x_refs, ck.raw(i), me_ref[0], eye_ref[...], scr, csh)
            xt = xt * (cm_ref[...] * rm_ref[at * step + i])
            r1 = lax.rsqrt(jnp.sum(xt * xt, axis=1, keepdims=True) / CH + EPS)
            u = (xt * r1 * g_ref[...]).astype(BF)
            ck.keep_orders(fs, i, mm(fb_ref[...], u))
            xt_ref[i] = xt.astype(BF)
        ck.write_orders(f_ref, fs)

    return pl.pallas_call(
        body,
        grid=ck.grid,
        in_specs=[SMEM]
        + [whole(fwd.shape), whole(eye.shape), whole(gain.shape), whole(cmask.shape), SMEM]
        + [pl.BlockSpec((step, cv, nlon), ck.row_map(0, 0))] * n,
        out_specs=[
            ck.order_spec(cp),
            pl.BlockSpec((step, nlon, cp), ck.row_map(0, 0)),
        ],
        out_shape=[
            ck.order_shape(cp),
            jax.ShapeDtypeStruct((ck.rows, nlon, cp), BF),
        ],
        scratch_shapes=[pltpu.VMEM((cp, nlon), F32), ck.order_scratch(cp)],
        compiler_params=params(48),
        name="fourier",
    )(me, fwd, eye, gain, cmask, row_mask, *grids)


def legendre(ck, data, table, n_dest, by_order, name):
    n_src, rows, cp = data.shape
    n_mi, n_out, n_in = table.shape
    inner = ck.inner
    out_each = n_out // n_dest
    tile = 256

    def body(x_ref, t_ref, o_ref, fin, fout):
        for d in range(n_src):
            spread(fin, d * rows, x_ref[d])
        for i in range(inner):
            got = pick_rows(fin, i, n_in, inner)
            res = mm(t_ref[(i // 2) % n_mi], got)
            at = i % ck.mk * ck.each + i // ck.mk if by_order and ck.left else i
            for d in range(n_dest):
                fout[d, at * out_each : (at + 1) * out_each] = res[d * out_each : (d + 1) * out_each]
        for d in range(n_dest):
            o_ref[d] = fout[d].astype(BF)

    return pl.pallas_call(
        body,
        grid=(cp // tile,),
        in_specs=[pl.BlockSpec((n_src, rows, tile), lambda c: (0, 0, c)), whole(table.shape)],
        out_specs=pl.BlockSpec((n_dest, inner * out_each, tile), lambda c: (0, 0, c)),
        out_shape=jax.ShapeDtypeStruct((n_dest, inner * out_each, cp), BF),
        scratch_shapes=[
            pltpu.VMEM((tile // LANE, n_src * rows, LANE), F32),
            pltpu.VMEM((n_dest, inner * out_each, tile), F32),
        ],
        compiler_params=params(56),
        name=name,
    )(data, table)


def mix(ck, coef, weights, csh, dims, name):
    n_sp, rows, cp = coef.shape
    n_tp, own, wrows, _ = weights.shape
    inner = ck.inner
    count = n_sp * inner
    qb = next((b for b in range(1, own + 1) if own % b == 0 and b * inner % 16 == 0), own)

    def body(x_ref, w_ref, o_ref, a_ref, fin, fout, wfull):
        k = pl.program_id(0)

        @pl.when(k == 0)
        def _():
            wfull[...] = jnp.zeros_like(wfull)
            for d in range(n_sp):
                spread(fin, d * rows, x_ref[d])

        for i in range(qb):
            a = pick_rows(fin, k * qb + i, count, own)
            a_ref[i] = a
            for t in range(n_tp):
                wfull[t * csh : t * csh + wrows] = w_ref[t, i]
            b = mm(a, wfull[...], dims)
            for d in range(n_sp):
                fout[d, i * inner : (i + 1) * inner] = b[d * inner : (d + 1) * inner]
        for d in range(n_sp):
            o_ref[d] = fout[d].astype(BF)

    return pl.pallas_call(
        body,
        grid=(own // qb,),
        in_specs=[
            whole(coef.shape),
            pl.BlockSpec((n_tp, qb, wrows, cp), lambda k: (0, k, 0, 0)),
        ],
        out_specs=[
            pl.BlockSpec((n_sp, qb * inner, cp), lambda k: (0, k, 0)),
            pl.BlockSpec((qb, count, cp), lambda k: (k, 0, 0)),
        ],
        out_shape=[
            jax.ShapeDtypeStruct((n_sp, own * inner, cp), BF),
            jax.ShapeDtypeStruct((own, count, cp), BF),
        ],
        scratch_shapes=[
            pltpu.VMEM((cp // LANE, n_sp * rows, LANE), F32),
            pltpu.VMEM((n_sp, qb * inner, cp), F32),
            pltpu.VMEM((n_tp * csh, cp), BF),
        ],
        compiler_params=params(56),
        name=name,
    )(coef, weights)


def weight_grads(grads, coefs, n_tp, wrows):
    n = len(grads)
    own, _, cp = grads[0].shape
    csh = cp // n_tp

    def body(*refs):
        o_ref = refs[-1]
        g = jnp.concatenate([r[0] for r in refs[:n]], axis=0)
        a = jnp.concatenate([r[0] for r in refs[n : 2 * n]], axis=0)
        dw = mm(g, a, TN)
        for t in range(n_tp):
            o_ref[t, 0] = dw[t * csh : t * csh + wrows].astype(BF)

    return pl.pallas_call(
        body,
        grid=(own,),
        in_specs=[pl.BlockSpec((1,) + v.shape[1:], lambda q: (q, 0, 0)) for v in grads + coefs],
        out_specs=pl.BlockSpec((n_tp, 1, wrows, cp), lambda q: (0, q, 0, 0)),
        out_shape=jax.ShapeDtypeStruct((n_tp, own, wrows, cp), BF),
        compiler_params=params(48),
        name="weight_grads",
    )(*grads, *coefs)


def grid_block(ck, coef, xt, cots, me, w_in, w_out, inv, inv_t, eye, gain, cmask, row_mask, csh):
    nd, _, rows_s, cp = coef.shape
    _, cv, nlon = cots[0].shape
    n = len(cots)
    hid = w_in.shape[0]
    rows, step, mk = ck.rows, ck.step, ck.mk
    jb = 2 if step % 2 == 0 else 1

    def body(me_ref, c_ref, xt_ref, wi_ref, wo_ref, ib_ref, it_ref, eye_ref, g_ref, cm_ref, rm_ref, *refs):
        ct_refs, out_refs = refs[:n], refs[n : 2 * n]
        dg_ref, dh_ref, dwi_ref, dwo_ref, gg_ref, fin, scr, oscr, hs, dms, fs = refs[2 * n :]
        k = pl.program_id(1)
        at = pl.program_id(0) * ck.blocks + k

        @pl.when(at == 0)
        def _():
            scr[...] = jnp.zeros_like(scr)
            dwi_ref[...] = jnp.zeros_like(dwi_ref)
            dwo_ref[...] = jnp.zeros_like(dwo_ref)
            gg_ref[...] = jnp.zeros_like(gg_ref)

        @pl.when(k == 0)
        def _():
            for d in range(nd):
                spread(fin, d * rows_s, c_ref[d, 0])

        for base in range(0, step, jb):
            for i in range(jb):
                r = base + i
                g = pick_rows(fin, k * ck.jb + ck.raw(r), nd * mk, ck.stride)
                hs[i] = xt_ref[r].astype(F32) + mm(it_ref[...], g)
                dm = load_transposed(ct_refs, ck.raw(r), me_ref[0], eye_ref[...], scr, csh)
                dms[i] = dm * (cm_ref[...] * rm_ref[at * step + r])
            h = jnp.concatenate([hs[i] for i in range(jb)], axis=0)
            dm = jnp.concatenate([dms[i] for i in range(jb)], axis=0)
            dmb = dm.astype(BF)
            r2 = lax.rsqrt(jnp.sum(h * h, axis=1, keepdims=True) / CH + EPS)
            g1 = g_ref[...]
            v = (h * r2 * g1).astype(BF)
            z = mm(v, wi_ref[...], NT)
            t = jnp.tanh(GELU_A * (z + GELU_B * z * z * z))
            act = (0.5 * z * (1.0 + t)).astype(BF)
            slope = 0.5 * (1.0 + t) + 0.5 * z * (1.0 - t * t) * (
                GELU_A * (1.0 + 3.0 * GELU_B * z * z)
            )
            out = (h + mm(act, wo_ref[...])).astype(BF)
            dz = (slope * mm(dmb, wo_ref[...], NT)).astype(BF)
            dwo_ref[...] += mm(act, dmb, TN)
            dwi_ref[...] += mm(dz, v, TN)
            dv = mm(dz, wi_ref[...])
            gd = g1 * dv
            proj = jnp.sum(h * gd, axis=1, keepdims=True) / CH
            dh = dm + r2 * gd - h * (r2 * r2 * r2 * proj)
            gg_ref[...] += jnp.sum(dv * h * r2, axis=0, keepdims=True)
            for i in range(jb):
                r = base + i
                part = dh[i * nlon : (i + 1) * nlon].astype(BF)
                dh_ref[r] = part
                ck.keep_orders(fs, r, mm(ib_ref[...], part))
                store_transposed(
                    out_refs, ck.raw(r), out[i * nlon : (i + 1) * nlon], me_ref[0], eye_ref[...], oscr, csh
                )
        ck.write_orders(dg_ref, fs)

    rowmap = ck.row_map(0, 0)
    fixed = lambda s, k: (0, 0)
    grid_spec = pl.BlockSpec((step, cv, nlon), rowmap)
    got = pl.pallas_call(
        body,
        grid=ck.grid,
        in_specs=[
            SMEM,
            ck.coef_spec(rows_s, cp),
            pl.BlockSpec((step, nlon, cp), rowmap),
            whole(w_in.shape),
            whole(w_out.shape),
            whole(inv.shape),
            whole(inv_t.shape),
            whole(eye.shape),
            whole(gain.shape),
            whole(cmask.shape),
            SMEM,
        ]
        + [grid_spec] * n,
        out_specs=[grid_spec] * n
        + [
            ck.order_spec(cp),
            pl.BlockSpec((step, nlon, cp), rowmap),
            pl.BlockSpec((hid, cp), fixed),
            pl.BlockSpec((hid, cp), fixed),
            pl.BlockSpec((1, cp), fixed),
        ],
        out_shape=[jax.ShapeDtypeStruct((rows, cv, nlon), BF)] * n
        + [
            ck.order_shape(cp),
            jax.ShapeDtypeStruct((rows, nlon, cp), BF),
            jax.ShapeDtypeStruct((hid, cp), F32),
            jax.ShapeDtypeStruct((hid, cp), F32),
            jax.ShapeDtypeStruct((1, cp), F32),
        ],
        scratch_shapes=[
            pltpu.VMEM((cp // LANE, nd * rows_s, LANE), F32),
            pltpu.VMEM((cp, nlon), F32),
            pltpu.VMEM((cp, nlon), F32),
            pltpu.VMEM((jb, nlon, cp), F32),
            pltpu.VMEM((jb, nlon, cp), F32),
            ck.order_scratch(cp),
        ],
        compiler_params=params(62),
        name="grid_block",
    )(me, coef, xt, w_in, w_out, inv, inv_t, eye, gain, cmask, row_mask, *cots)
    return got[:n], got[n:]


def grid_final(ck, coef, xt, dh, me, fwd_t, eye, gain, cmask, row_mask, csh, n, cv):
    nd, _, rows_s, cp = coef.shape
    rows, nlon, _ = xt.shape
    step, mk = ck.step, ck.mk

    def body(me_ref, c_ref, xt_ref, dh_ref, ft_ref, eye_ref, g_ref, cm_ref, rm_ref, *refs):
        out_refs, (gg_ref, fin, oscr) = refs[:n], refs[n:]
        k = pl.program_id(1)
        at = pl.program_id(0) * ck.blocks + k

        @pl.when(at == 0)
        def _():
            gg_ref[...] = jnp.zeros_like(gg_ref)

        @pl.when(k == 0)
        def _():
            for d in range(nd):
                spread(fin, d * rows_s, c_ref[d, 0])

        for i in range(step):
            du = mm(ft_ref[...], pick_rows(fin, k * ck.jb + ck.raw(i), nd * mk, ck.stride))
            x = xt_ref[i].astype(F32)
            r1 = lax.rsqrt(jnp.sum(x * x, axis=1, keepdims=True) / CH + EPS)
            gd = g_ref[...] * du
            proj = jnp.sum(x * gd, axis=1, keepdims=True) / CH
            res = dh_ref[i].astype(F32) + r1 * gd - x * (r1 * r1 * r1 * proj)
            res = (res * (cm_ref[...] * rm_ref[at * step + i])).astype(BF)
            gg_ref[...] += jnp.sum(du * x * r1, axis=0, keepdims=True)
            store_transposed(out_refs, ck.raw(i), res, me_ref[0], eye_ref[...], oscr, csh)

    rowmap = ck.row_map(0, 0)
    got = pl.pallas_call(
        body,
        grid=ck.grid,
        in_specs=[
            SMEM,
            ck.coef_spec(rows_s, cp),
            pl.BlockSpec((step, nlon, cp), rowmap),
            pl.BlockSpec((step, nlon, cp), rowmap),
            whole(fwd_t.shape),
            whole(eye.shape),
            whole(gain.shape),
            whole(cmask.shape),
            SMEM,
        ],
        out_specs=[pl.BlockSpec((step, cv, nlon), rowmap)] * n
        + [pl.BlockSpec((1, cp), lambda s, k: (0, 0))],
        out_shape=[jax.ShapeDtypeStruct((rows, cv, nlon), BF)] * n
        + [jax.ShapeDtypeStruct((1, cp), F32)],
        scratch_shapes=[
            pltpu.VMEM((cp // LANE, nd * rows_s, LANE), F32),
            pltpu.VMEM((cp, nlon), F32),
        ],
        compiler_params=params(48),
        name="grid_final",
    )(me, coef, xt, dh, fwd_t, eye, gain, cmask, row_mask)
    return got[:n], got[n]


def adamw(param, grad, first, second, rate, decay):
    new_first = 0.5 * first + 0.5 * grad
    new_second = 0.5 * second + 0.5 * grad * grad
    update = new_first / BIAS_FIX / (jnp.sqrt(new_second / BIAS_FIX) + ADAM_EPS)
    return (param - rate * (update + decay * param), new_first, new_second)


def swap(value, axis):
    return lax.all_to_all(value, axis, split_axis=0, concat_axis=0, tiled=True)


def after(value, *others):
    return lax.optimization_barrier((value, others))[0]


def local(
    n_sp, n_tp,
    state, cotangent, rollout_lengths, channel_sizes, owner_slots,
    master, first_moment, second_moment, gains, gain_first, gain_second,
):
    slots, latd, flat = state.shape
    own, csh, cp = master.shape
    nlon = flat // csh
    sp, tp = lax.axis_index("sp"), lax.axis_index("tp")
    me = tp.astype(jnp.int32).reshape(1)
    degrees = owner_slots.shape[0] - 4
    n_mi = (degrees + n_sp - 1) // n_sp
    mpad = n_mi * n_sp
    plan = Plan(slots, latd, n_sp, n_tp, n_mi)
    chunks = plan.chunks
    nlatp = latd * n_sp
    valid = CVALID * nlon
    tile = 19 * 128
    lanes = pl.cdiv(valid, tile) * tile

    fwd, inv, analysis, synthesis = tables(NLAT, nlatp, nlon, degrees, mpad)
    fwd_t, inv_t = jnp.asarray(fwd.T), jnp.asarray(inv.T)
    fwd, inv = jnp.asarray(fwd), jnp.asarray(inv)
    eye = jnp.asarray(np.eye(nlon).astype(ml_dtypes.bfloat16))
    pick = (owner_slots[:degrees, None] == jnp.arange(n_sp * own)[None, :]).astype(BF)
    mine = lambda t: lax.dynamic_slice_in_dim(jnp.asarray(t), sp * n_mi, n_mi, 0)
    by_slot = lambda t: jnp.einsum("mlj,lq->mqj", mine(t), pick, preferred_element_type=F32).astype(BF)
    ana_q, syn_q = by_slot(analysis), by_slot(synthesis)
    ana_j, syn_j = jnp.swapaxes(ana_q, 1, 2), jnp.swapaxes(syn_q, 1, 2)

    def table(ck, t):
        return t if ck.nm == n_mi else lax.dynamic_slice_in_dim(t, tp * ck.nm, ck.nm, 0)

    chan = jnp.arange(cp)
    cmask = (chan % csh < channel_sizes[chan // csh]).astype(F32)
    rmask = (jnp.arange(csh) < channel_sizes[tp]).astype(F32)
    cmask2 = cmask[None, :]
    samples = rollout_lengths.shape[0]
    row_masks, cot_masks = [], []
    for ck in chunks:
        first, lat0 = (n_tp * plan.main, tp * ck.jn) if ck.left else (tp * plan.main, 0)
        ids = first + jnp.arange(ck.each)
        live = ids % ROLL < rollout_lengths[jnp.minimum(ids // ROLL, samples - 1)]
        live = (live & (ids < slots)).astype(F32)
        lat = (sp * latd + lat0 + jnp.arange(ck.jn) < NLAT).astype(F32)
        masks = jnp.ones((ck.each, 1), F32) * lat[None, :], live[:, None] * lat[None, :]
        masks = [(m.T if ck.left else m).reshape(-1) for m in masks]
        row_masks.append(masks[0])
        cot_masks.append(masks[1])

    copies = (master * (rmask[:, None] * cmask2)[None]).astype(BF)
    hrow = (jnp.arange(2 * csh) < 2 * channel_sizes[tp]).astype(F32).reshape(2, csh)
    raw = []
    for i in range(4):
        at = owner_slots[degrees + i] - sp * own
        inside = (at >= 0) & (at < own)
        piece = lax.dynamic_index_in_dim(master, jnp.clip(at, 0, own - 1), 0, keepdims=False)
        keep = hrow[i % 2][:, None] * cmask2 * inside.astype(F32)
        raw.append((piece * keep).astype(BF))
    gains_all = swap(jnp.broadcast_to(gains[None], (n_tp,) + gains.shape), "tp")
    gains_all = jnp.swapaxes(gains_all, 0, 1).reshape(2, cp)

    cut = lambda a: a[:, :valid].reshape(-1, CVALID, nlon)
    flat_of = lambda a: jnp.pad(a.reshape(a.shape[0], valid), ((0, 0), (0, lanes - valid)))
    send = lambda a, d: lax.ppermute(a, "tp", [(i, i ^ d) for i in range(n_tp)]) if d else a
    send_all = lambda arrays: [send(a, d) for d, a in enumerate(arrays)]
    rows3 = lambda v: v.reshape(v.shape[0], -1, cp)

    turn = []

    def swap_next(value, axes, *ties):
        out = swap(after(value, *turn, *ties), axes)
        turn[:] = [out]
        return out

    main, left = pack_rows(state, me, plan, lanes, tile)
    main = send_all(after(main, gains_all))
    left = send_all(after(left, main[1])) if left else []
    main, left = [cut(a) for a in main], [cut(a) for a in left]
    x5 = [main, left]
    spec_w = lax.all_gather(after(copies[:, :CROWS], main, gains_all), "tp", axis=0, tiled=False)
    gain_a, gain_b = gains_all[:1], gains_all[1:]
    n = len(chunks)
    odd = lambda arrays: [send(a, d) if d % 2 else a for d, a in enumerate(arrays)]
    even = lambda arrays: [a if d % 2 else send(a, d) for d, a in enumerate(arrays)]

    fs, xts = [], []
    for i, ck in enumerate(chunks):
        f, xt = fourier(ck, x5[i], me, fwd, eye, gain_a, cmask2, row_masks[i], csh)
        xts.append(xt)
        if i == 1:
            fs[0] = after(fs[0], f)
        fs.append(swap_next(rows3(f), ck.axes))
    dense = lax.psum_scatter(after(jnp.stack(raw), fs[0]), "sp", scatter_dimension=1, tiled=True)
    coefs = []
    for f, ck in zip(fs, chunks):
        c = legendre(ck, f, table(ck, ana_q), n_sp, False, "analysis")
        coefs.append(swap_next(c, "sp", *((spec_w,) if ck.left else ())))
    coefs[0] = after(coefs[0], dense)
    dense = lax.all_gather(after(dense, coefs[0]), "tp", axis=1, tiled=False)
    m, a = mix(chunks[0], coefs[0], spec_w, csh, NT, "mix_forward")
    mixed, coef_q = [swap_next(m, "sp")], [a]
    main, left = pack_rows(after(cotangent, m, dense), me, plan, lanes, tile)
    ahead = odd(main)
    if n > 1:
        m, a = mix(chunks[1], after(coefs[1], main), spec_w, csh, NT, "mix_forward")
        mixed.append(swap_next(m, "sp", ahead))
        coef_q.append(a)
    dense = lax.all_gather(after(dense, mixed[0]), "sp", axis=2, tiled=True)
    w_in = dense[:2].reshape(2 * cp, cp)
    w_out = dense[2:].reshape(2 * cp, cp)
    main, left = after((ahead, left), mixed[0])
    main, left = even(main), send_all(left)
    synth = []
    for i, ck in enumerate(chunks):
        g = legendre(ck, mixed[i], table(ck, syn_j), ck.nd, True, "synthesis")
        synth.append(ck.grid_coef(swap_next(g, ck.axes, *((main, left) if i else ()))))
    cot5 = [[cut(a) for a in main], [cut(a) for a in left]]
    outs, rest, dgs = [], [], []
    for i, ck in enumerate(chunks):
        o, r = grid_block(
            ck, synth[i], xts[i], cot5[i], me, w_in, w_out, inv, inv_t, eye, gain_b, cmask2,
            cot_masks[i], csh,
        )
        outs.append([flat_of(a) for a in o])
        rest.append(r)
        if i == 0:
            dgs.append(swap_next(rows3(r[0]), ck.axes))
            main = odd(outs[0])
        else:
            dgs.append(swap_next(rows3(r[0]), ck.axes, main))
    left = outs[1] if n > 1 else []
    dbs = []
    for i, ck in enumerate(chunks):
        g = legendre(ck, dgs[i], table(ck, syn_q), n_sp, False, "synthesis_back")
        if i == 0:
            main, left = after((main, left), g)
            main, left = even(main), send_all(left)
            dbs.append(swap_next(g, "sp"))
        else:
            dbs.append(swap_next(g, "sp", main))
    das, grad_q = [], []
    for ck, b in zip(chunks, dbs):
        a, g = mix(ck, b, spec_w, csh, NN, "mix_backward")
        das.append(swap_next(a, "sp", *((left,) if ck.left else ())))
        grad_q.append(g)
    pieces_out = [(0, main)] + ([(-1, left)] if left else [])
    result = unpack_rows(pieces_out, me, plan, flat, valid, lanes, tile)
    dws = weight_grads(grad_q, coef_q, n_tp, CROWS)
    das[0] = after(das[0], dws)
    dfs = []
    for ck, a in zip(chunks, das):
        g = legendre(ck, a, table(ck, ana_j), ck.nd, True, "analysis_back")
        dfs.append(swap_next(g, ck.axes))
    half = own // 2
    scatter = lambda v: lax.psum_scatter(v, "tp", scatter_dimension=0, tiled=False)
    spec_a = scatter(after(dws[:, :half], pieces_out))
    dfs[0] = after(dfs[0], spec_a)
    spec_b = scatter(after(dws[:, half:], spec_a))
    dfs[-1] = after(dfs[-1], spec_b)
    spec_g = jnp.concatenate([spec_a, spec_b], axis=0)
    pieces, gg_a = [], 0.0
    for i, ck in enumerate(chunks):
        o, gg = grid_final(
            ck, ck.grid_coef(dfs[i]), xts[i], rest[i][1], me, fwd_t, eye, gain_a, cmask2,
            row_masks[i], csh, n_tp, CVALID,
        )
        gg_a = gg_a + gg
        pieces.append((-1 if ck.left else 0, send_all([flat_of(a) for a in o])))

    dwi = sum(r[2] for r in rest)
    dwo = sum(r[3] for r in rest)
    gg_b = sum(r[4] for r in rest)
    dense_g = jnp.stack([dwi, dwo]).reshape(4, n_tp, csh, cp).astype(BF)
    dense_g = lax.psum_scatter(after(dense_g, dgs[0]), "sp", scatter_dimension=2, tiled=True)
    dense_g = lax.psum_scatter(after(dense_g, das[0]), "tp", scatter_dimension=1, tiled=False)
    dense_g = lax.all_gather(after(dense_g, dfs[0]), "sp", axis=1, tiled=True).astype(F32)
    spec_g = jnp.pad(spec_g.astype(F32), ((0, 0), (0, csh - CROWS), (0, 0)))
    grads = spec_g
    for i in range(4):
        hit = (owner_slots[degrees + i] == sp * own + jnp.arange(own))[:, None, None]
        grads = jnp.where(hit, dense_g[i][None], grads)
    new_master, new_first, new_second = adamw(master, grads, first_moment, second_moment, 0.03, 0.01)
    gain_g = lax.psum(after(jnp.concatenate([gg_a, gg_b], axis=0), new_master), ("sp", "tp"))
    gain_g = lax.dynamic_slice_in_dim(gain_g, tp * csh, csh, 1)
    new_gains, gain_one, gain_two = adamw(gains, gain_g, gain_first, gain_second, 0.5, 0.0)
    grad_state = unpack_rows(
        pieces, after(me, new_gains, new_master), plan, flat, valid, lanes, tile
    )
    return (
        result, grad_state, new_master, new_master.astype(BF), new_first, new_second,
        new_gains, gain_one, gain_two,
    )


def solution(mesh):
    wide, slot, gain = P(None, "sp", "tp"), P("sp", "tp", None), P(None, "tp")
    return jax.shard_map(
        functools.partial(local, mesh.shape["sp"], mesh.shape["tp"]),
        mesh=mesh,
        in_specs=(wide, wide, P(), P(), P(), slot, slot, slot, gain, gain, gain),
        out_specs=(wide, wide, slot, slot, slot, slot, gain, gain, gain),
        check_vma=False,
    )
```

```python
import functools
import math

import jax
import jax.numpy as jnp
import ml_dtypes
import numpy as np
from jax import lax
from jax.experimental import pallas as pl
from jax.experimental.pallas import tpu as pltpu
from jax.sharding import PartitionSpec as P

CH = 641
CVALID = 161
CROWS = 168
NLAT = 90
ROLL = 5
EPS = 1e-05
ADAM_EPS = 1e-08
BIAS_FIX = 1.0 - 0.5**5
GELU_A = math.sqrt(2.0 / math.pi)
GELU_B = 0.044715
BF = jnp.bfloat16
F32 = jnp.float32
NT = (((1,), (1,)), ((), ()))
NN = (((1,), (0,)), ((), ()))
TN = (((0,), (0,)), ((), ()))


def mm(a, b, dims=NN):
    return lax.dot_general(a, b, dims, preferred_element_type=F32)


def tables(nlat, nlatp, nlon, mmax, mpad):
    theta = (np.arange(nlat) + 0.5) * (math.pi / nlat)
    cosine, sine = np.cos(theta), np.sin(theta)
    legendre = np.zeros((mmax, mmax, nlat))
    for m in range(mmax):
        value = math.sqrt(0.5) * np.ones(nlat)
        for k in range(1, m + 1):
            value = value * math.sqrt((2 * k + 1) / (2 * k)) * sine
        legendre[m, m] = value
        if m + 1 < mmax:
            legendre[m, m + 1] = math.sqrt(2 * m + 3) * cosine * value
        for l in range(m + 2, mmax):
            a = math.sqrt((4 * l * l - 1) / (l * l - m * m))
            b = math.sqrt(((l - 1) ** 2 - m * m) / (4 * (l - 1) ** 2 - 1))
            legendre[m, l] = a * (cosine * legendre[m, l - 1] - b * legendre[m, l - 2])
    analysis = np.zeros((mpad, mmax, nlatp))
    synthesis = np.zeros((mpad, mmax, nlatp))
    analysis[:mmax, :, :nlat] = legendre * sine * (math.pi / nlat)
    synthesis[:mmax, :, :nlat] = legendre
    angle = (np.arange(mmax)[:, None] * np.arange(nlon)[None, :] % nlon) * (2.0 * math.pi / nlon)
    fwd = np.zeros((mpad, 2, nlon))
    fwd[:mmax, 0] = np.cos(angle) * math.sqrt(2.0 / nlon)
    fwd[:mmax, 1] = -np.sin(angle) * math.sqrt(2.0 / nlon)
    fwd_low = fwd.astype(np.float32).astype(ml_dtypes.bfloat16)
    inv = fwd.copy()
    inv[0] *= 0.5
    inv_low = inv.astype(np.float32).astype(ml_dtypes.bfloat16)
    low = lambda v: v.astype(np.float32).astype(ml_dtypes.bfloat16)
    return (
        fwd_low.reshape(mpad * 2, nlon),
        inv_low.reshape(mpad * 2, nlon),
        low(analysis),
        low(synthesis),
    )


def params(mib):
    return pltpu.CompilerParams(vmem_limit_bytes=mib * 2**20)


def whole(shape):
    return pl.BlockSpec(shape, lambda *_: (0,) * len(shape), pipeline_mode=pl.Buffered(1))


SMEM = pl.BlockSpec(memory_space=pltpu.SMEM)


LANE = 128


def spread(scr, start, value):
    rows, cols = value.shape
    for t in range(cols // LANE):
        scr[t, start : start + rows, :] = value[:, t * LANE : (t + 1) * LANE].astype(F32)


def pick_rows(scr, start, count, stride):
    parts = [scr[t, pl.ds(start, count, stride=stride), :] for t in range(scr.shape[0])]
    return jnp.concatenate(parts, axis=1).astype(BF)


class Plan:
    def __init__(self, slots, latd, n_sp, n_tp, n_mi):
        left = slots % n_tp
        self.split = left > 0 and latd % n_tp == 0 and n_mi % n_tp == 0
        self.slots, self.latd, self.n_tp = slots, latd, n_tp
        self.main = slots // n_tp if self.split else -(-slots // n_tp)
        self.left = left if self.split else 0
        self.part = latd // n_tp if self.split else 0
        self.chunks = [Chunk(self.main, latd, n_sp, n_mi, "sp", False)]
        if self.split:
            self.chunks.append(
                Chunk(left, self.part, n_sp * n_tp, n_mi // n_tp, ("sp", "tp"), True)
            )


class Chunk:
    def __init__(self, each, jn, nd, nm, axes, left):
        self.each, self.jn, self.nd, self.nm, self.axes, self.left = each, jn, nd, nm, axes, left
        self.rows = each * jn
        self.mk = 2 * nm
        self.inner = each * self.mk
        self.jb = 2 if jn % 2 == 0 else 1
        self.step = self.rows if left else self.jb
        self.blocks = 1 if left else jn // self.jb
        self.grid = (1, 1) if left else (each, self.blocks)
        self.stride = self.rows if left else jn

    def raw(self, i):
        return (i % self.each) * self.jn + i // self.each if self.left else i

    def row_map(self, *rest):
        return lambda s, k: (s * self.blocks + k,) + rest

    def order_spec(self, cp):
        if self.left:
            return pl.BlockSpec((self.nd, self.rows * self.mk, cp), lambda s, k: (0, 0, 0))
        return pl.BlockSpec((self.nd, self.jb, 1, self.mk, cp), lambda s, k: (0, k, s, 0, 0))

    def order_shape(self, cp):
        if self.left:
            return jax.ShapeDtypeStruct((self.nd, self.rows * self.mk, cp), BF)
        return jax.ShapeDtypeStruct((self.nd, self.jn, self.each, self.mk, cp), BF)

    def order_scratch(self, cp):
        return pltpu.VMEM((self.nd, self.step * self.mk, cp), F32)

    def keep_orders(self, fs, i, value):
        for d in range(self.nd):
            fs[d, i * self.mk : (i + 1) * self.mk] = value[d * self.mk : (d + 1) * self.mk]

    def write_orders(self, ref, fs):
        for d in range(self.nd):
            if self.left:
                ref[d] = fs[d].astype(BF)
            else:
                for i in range(self.step):
                    ref[d, i, 0] = fs[d, i * self.mk : (i + 1) * self.mk].astype(BF)

    def grid_coef(self, value):
        return value.reshape(self.nd, self.grid[0], -1, value.shape[-1])

    def coef_spec(self, rows_s, cp):
        return pl.BlockSpec((self.nd, 1, rows_s, cp), lambda s, k: (0, s, 0, 0))


def pack_rows(state, me, plan, lanes, tile):
    slots, latd, _ = state.shape
    n_tp, main, left, part = plan.n_tp, plan.main, plan.left, plan.part

    def body(me_ref, x_ref, *outs):
        for d in range(n_tp):
            t = me_ref[0] ^ d
            parts = []
            for i in range(main):
                at = t * main + i
                v = x_ref[jnp.minimum(at, slots - 1)].astype(F32)
                parts.append(jnp.where(at < slots, v, 0.0) if n_tp * main > slots else v)
            outs[d][...] = jnp.concatenate(parts, axis=0).astype(BF)
        if left:
            whole_rows = [x_ref[n_tp * main + i].astype(F32) for i in range(left)]
            options = [
                jnp.concatenate([v[t * part : (t + 1) * part] for v in whole_rows], axis=0)
                for t in range(n_tp)
            ]
            for d in range(n_tp):
                t = me_ref[0] ^ d
                acc = options[0]
                for o in range(1, n_tp):
                    acc = jnp.where(t == o, options[o], acc)
                outs[n_tp + d][...] = acc.astype(BF)

    counts = [main * latd] * n_tp + [left * part] * (n_tp if left else 0)
    got = pl.pallas_call(
        body,
        grid=(lanes // tile,),
        in_specs=[SMEM, pl.BlockSpec((slots, latd, tile), lambda l: (0, 0, l))],
        out_specs=[pl.BlockSpec((c, tile), lambda l: (0, l)) for c in counts],
        out_shape=[jax.ShapeDtypeStruct((c, lanes), BF) for c in counts],
        compiler_params=params(32),
        name="pack_rows",
    )(me, state)
    return got[:n_tp], got[n_tp:]


def unpack_rows(pieces, me, plan, flat, valid, lanes, tile):
    slots, latd, n_tp, main, left, part = (
        plan.slots, plan.latd, plan.n_tp, plan.main, plan.left, plan.part,
    )
    last = lanes // tile - 1
    arrays = [a for _, group in pieces for a in group]

    def body(me_ref, *refs):
        o_ref = refs[-1]
        lane = pl.program_id(0) * tile + lax.broadcasted_iota(jnp.int32, (1, tile), 1)
        keep = lane < valid
        for p, (first, _) in enumerate(pieces):
            group = refs[p * n_tp : (p + 1) * n_tp]
            values = [jnp.where(keep, g[...].astype(F32), 0.0) for g in group]
            if first >= 0:
                for d in range(n_tp):
                    for i in range(values[d].shape[0] // latd):
                        at = (me_ref[0] ^ d) * main + first + i

                        @pl.when(at < slots)
                        def _(at=at, d=d, i=i):
                            o_ref[at] = values[d][i * latd : (i + 1) * latd].astype(BF)
            else:
                ordered = []
                for t in range(n_tp):
                    acc = values[0]
                    for d in range(1, n_tp):
                        acc = jnp.where((me_ref[0] ^ d) == t, values[d], acc)
                    ordered.append(acc)
                for i in range(left):
                    o_ref[n_tp * main + i] = jnp.concatenate(
                        [v[i * part : (i + 1) * part] for v in ordered], axis=0
                    ).astype(BF)

    return pl.pallas_call(
        body,
        grid=(pl.cdiv(flat, tile),),
        in_specs=[SMEM]
        + [pl.BlockSpec((a.shape[0], tile), lambda l: (0, jnp.minimum(l, last))) for a in arrays],
        out_specs=pl.BlockSpec((slots, latd, tile), lambda l: (0, 0, l)),
        out_shape=jax.ShapeDtypeStruct((slots, latd, flat), BF),
        compiler_params=params(48),
        name="unpack_rows",
    )(me, *arrays)


def load_transposed(refs, row, me, eye, scr, csh):
    for d, ref in enumerate(refs):
        start = pl.multiple_of((me ^ d) * csh, 64)
        scr[pl.ds(start, ref.shape[1]), :] = ref[row].astype(F32)
    return mm(eye, scr[...].astype(BF), NT)


def store_transposed(refs, row, value, me, eye, scr, csh):
    scr[...] = mm(value, eye, TN)
    for d, ref in enumerate(refs):
        start = pl.multiple_of((me ^ d) * csh, 64)
        ref[row] = scr[pl.ds(start, ref.shape[1]), :].astype(BF)


def fourier(ck, grids, me, fwd, eye, gain, cmask, row_mask, csh):
    _, cv, nlon = grids[0].shape
    n = len(grids)
    cp = cmask.shape[1]
    step = ck.step

    def body(me_ref, fb_ref, eye_ref, g_ref, cm_ref, rm_ref, *refs):
        x_refs, (f_ref, xt_ref, scr, fs) = refs[:n], refs[n:]
        at = pl.program_id(0) * ck.blocks + pl.program_id(1)

        @pl.when(at == 0)
        def _():
            scr[...] = jnp.zeros_like(scr)

        for i in range(step):
            xt = load_transposed(x_refs, ck.raw(i), me_ref[0], eye_ref[...], scr, csh)
            xt = xt * (cm_ref[...] * rm_ref[at * step + i])
            r1 = lax.rsqrt(jnp.sum(xt * xt, axis=1, keepdims=True) / CH + EPS)
            u = (xt * r1 * g_ref[...]).astype(BF)
            ck.keep_orders(fs, i, mm(fb_ref[...], u))
            xt_ref[i] = xt.astype(BF)
        ck.write_orders(f_ref, fs)

    return pl.pallas_call(
        body,
        grid=ck.grid,
        in_specs=[SMEM]
        + [whole(fwd.shape), whole(eye.shape), whole(gain.shape), whole(cmask.shape), SMEM]
        + [pl.BlockSpec((step, cv, nlon), ck.row_map(0, 0))] * n,
        out_specs=[
            ck.order_spec(cp),
            pl.BlockSpec((step, nlon, cp), ck.row_map(0, 0)),
        ],
        out_shape=[
            ck.order_shape(cp),
            jax.ShapeDtypeStruct((ck.rows, nlon, cp), BF),
        ],
        scratch_shapes=[pltpu.VMEM((cp, nlon), F32), ck.order_scratch(cp)],
        compiler_params=params(48),
        name="fourier",
    )(me, fwd, eye, gain, cmask, row_mask, *grids)


def legendre(ck, data, table, n_dest, by_order, name):
    n_src, rows, cp = data.shape
    n_mi, n_out, n_in = table.shape
    inner = ck.inner
    out_each = n_out // n_dest
    tile = 256

    def body(x_ref, t_ref, o_ref, fin, fout):
        for d in range(n_src):
            spread(fin, d * rows, x_ref[d])
        for i in range(inner):
            got = pick_rows(fin, i, n_in, inner)
            res = mm(t_ref[(i // 2) % n_mi], got)
            at = i % ck.mk * ck.each + i // ck.mk if by_order and ck.left else i
            for d in range(n_dest):
                fout[d, at * out_each : (at + 1) * out_each] = res[d * out_each : (d + 1) * out_each]
        for d in range(n_dest):
            o_ref[d] = fout[d].astype(BF)

    return pl.pallas_call(
        body,
        grid=(cp // tile,),
        in_specs=[pl.BlockSpec((n_src, rows, tile), lambda c: (0, 0, c)), whole(table.shape)],
        out_specs=pl.BlockSpec((n_dest, inner * out_each, tile), lambda c: (0, 0, c)),
        out_shape=jax.ShapeDtypeStruct((n_dest, inner * out_each, cp), BF),
        scratch_shapes=[
            pltpu.VMEM((tile // LANE, n_src * rows, LANE), F32),
            pltpu.VMEM((n_dest, inner * out_each, tile), F32),
        ],
        compiler_params=params(56),
        name=name,
    )(data, table)


def mix(ck, coef, weights, csh, dims, name):
    n_sp, rows, cp = coef.shape
    n_tp, own, wrows, _ = weights.shape
    inner = ck.inner
    count = n_sp * inner
    qb = next((b for b in range(1, own + 1) if own % b == 0 and b * inner % 16 == 0), own)

    def body(x_ref, w_ref, o_ref, a_ref, fin, fout, wfull):
        k = pl.program_id(0)

        @pl.when(k == 0)
        def _():
            wfull[...] = jnp.zeros_like(wfull)
            for d in range(n_sp):
                spread(fin, d * rows, x_ref[d])

        for i in range(qb):
            a = pick_rows(fin, k * qb + i, count, own)
            a_ref[i] = a
            for t in range(n_tp):
                wfull[t * csh : t * csh + wrows] = w_ref[t, i]
            b = mm(a, wfull[...], dims)
            for d in range(n_sp):
                fout[d, i * inner : (i + 1) * inner] = b[d * inner : (d + 1) * inner]
        for d in range(n_sp):
            o_ref[d] = fout[d].astype(BF)

    return pl.pallas_call(
        body,
        grid=(own // qb,),
        in_specs=[
            whole(coef.shape),
            pl.BlockSpec((n_tp, qb, wrows, cp), lambda k: (0, k, 0, 0)),
        ],
        out_specs=[
            pl.BlockSpec((n_sp, qb * inner, cp), lambda k: (0, k, 0)),
            pl.BlockSpec((qb, count, cp), lambda k: (k, 0, 0)),
        ],
        out_shape=[
            jax.ShapeDtypeStruct((n_sp, own * inner, cp), BF),
            jax.ShapeDtypeStruct((own, count, cp), BF),
        ],
        scratch_shapes=[
            pltpu.VMEM((cp // LANE, n_sp * rows, LANE), F32),
            pltpu.VMEM((n_sp, qb * inner, cp), F32),
            pltpu.VMEM((n_tp * csh, cp), BF),
        ],
        compiler_params=params(56),
        name=name,
    )(coef, weights)


def weight_grads(grads, coefs, n_tp, wrows, first, own):
    n = len(grads)
    cp = grads[0].shape[2]
    csh = cp // n_tp

    def body(*refs):
        o_ref = refs[-1]
        g = jnp.concatenate([r[0] for r in refs[:n]], axis=0)
        a = jnp.concatenate([r[0] for r in refs[n : 2 * n]], axis=0)
        dw = mm(g, a, TN)
        for t in range(n_tp):
            o_ref[t, 0] = dw[t * csh : t * csh + wrows].astype(BF)

    return pl.pallas_call(
        body,
        grid=(own,),
        in_specs=[
            pl.BlockSpec((1,) + v.shape[1:], lambda q: (q + first, 0, 0)) for v in grads + coefs
        ],
        out_specs=pl.BlockSpec((n_tp, 1, wrows, cp), lambda q: (0, q, 0, 0)),
        out_shape=jax.ShapeDtypeStruct((n_tp, own, wrows, cp), BF),
        compiler_params=params(48),
        name="weight_grads",
    )(*grads, *coefs)


def grid_block(ck, coef, xt, cots, me, w_in, w_out, inv, inv_t, eye, gain, cmask, row_mask, csh):
    nd, _, rows_s, cp = coef.shape
    _, cv, nlon = cots[0].shape
    n = len(cots)
    hid = w_in.shape[0]
    rows, step, mk = ck.rows, ck.step, ck.mk
    jb = 2 if step % 2 == 0 else 1

    def body(me_ref, c_ref, xt_ref, wi_ref, wo_ref, ib_ref, it_ref, eye_ref, g_ref, cm_ref, rm_ref, *refs):
        ct_refs, out_refs = refs[:n], refs[n : 2 * n]
        dg_ref, dh_ref, dwi_ref, dwo_ref, gg_ref, fin, scr, oscr, hs, dms, fs = refs[2 * n :]
        k = pl.program_id(1)
        at = pl.program_id(0) * ck.blocks + k

        @pl.when(at == 0)
        def _():
            scr[...] = jnp.zeros_like(scr)
            dwi_ref[...] = jnp.zeros_like(dwi_ref)
            dwo_ref[...] = jnp.zeros_like(dwo_ref)
            gg_ref[...] = jnp.zeros_like(gg_ref)

        @pl.when(k == 0)
        def _():
            for d in range(nd):
                spread(fin, d * rows_s, c_ref[d, 0])

        for base in range(0, step, jb):
            for i in range(jb):
                r = base + i
                g = pick_rows(fin, k * ck.jb + ck.raw(r), nd * mk, ck.stride)
                hs[i] = xt_ref[r].astype(F32) + mm(it_ref[...], g)
                dm = load_transposed(ct_refs, ck.raw(r), me_ref[0], eye_ref[...], scr, csh)
                dms[i] = dm * (cm_ref[...] * rm_ref[at * step + r])
            h = jnp.concatenate([hs[i] for i in range(jb)], axis=0)
            dm = jnp.concatenate([dms[i] for i in range(jb)], axis=0)
            dmb = dm.astype(BF)
            r2 = lax.rsqrt(jnp.sum(h * h, axis=1, keepdims=True) / CH + EPS)
            g1 = g_ref[...]
            v = (h * r2 * g1).astype(BF)
            z = mm(v, wi_ref[...], NT)
            t = jnp.tanh(GELU_A * (z + GELU_B * z * z * z))
            act = (0.5 * z * (1.0 + t)).astype(BF)
            slope = 0.5 * (1.0 + t) + 0.5 * z * (1.0 - t * t) * (
                GELU_A * (1.0 + 3.0 * GELU_B * z * z)
            )
            out = (h + mm(act, wo_ref[...])).astype(BF)
            dz = (slope * mm(dmb, wo_ref[...], NT)).astype(BF)
            dwo_ref[...] += mm(act, dmb, TN)
            dwi_ref[...] += mm(dz, v, TN)
            dv = mm(dz, wi_ref[...])
            gd = g1 * dv
            proj = jnp.sum(h * gd, axis=1, keepdims=True) / CH
            dh = dm + r2 * gd - h * (r2 * r2 * r2 * proj)
            gg_ref[...] += jnp.sum(dv * h * r2, axis=0, keepdims=True)
            for i in range(jb):
                r = base + i
                part = dh[i * nlon : (i + 1) * nlon].astype(BF)
                dh_ref[r] = part
                ck.keep_orders(fs, r, mm(ib_ref[...], part))
                store_transposed(
                    out_refs, ck.raw(r), out[i * nlon : (i + 1) * nlon], me_ref[0], eye_ref[...], oscr, csh
                )
        ck.write_orders(dg_ref, fs)

    rowmap = ck.row_map(0, 0)
    fixed = lambda s, k: (0, 0)
    grid_spec = pl.BlockSpec((step, cv, nlon), rowmap)
    got = pl.pallas_call(
        body,
        grid=ck.grid,
        in_specs=[
            SMEM,
            ck.coef_spec(rows_s, cp),
            pl.BlockSpec((step, nlon, cp), rowmap),
            whole(w_in.shape),
            whole(w_out.shape),
            whole(inv.shape),
            whole(inv_t.shape),
            whole(eye.shape),
            whole(gain.shape),
            whole(cmask.shape),
            SMEM,
        ]
        + [grid_spec] * n,
        out_specs=[grid_spec] * n
        + [
            ck.order_spec(cp),
            pl.BlockSpec((step, nlon, cp), rowmap),
            pl.BlockSpec((hid, cp), fixed),
            pl.BlockSpec((hid, cp), fixed),
            pl.BlockSpec((1, cp), fixed),
        ],
        out_shape=[jax.ShapeDtypeStruct((rows, cv, nlon), BF)] * n
        + [
            ck.order_shape(cp),
            jax.ShapeDtypeStruct((rows, nlon, cp), BF),
            jax.ShapeDtypeStruct((hid, cp), F32),
            jax.ShapeDtypeStruct((hid, cp), F32),
            jax.ShapeDtypeStruct((1, cp), F32),
        ],
        scratch_shapes=[
            pltpu.VMEM((cp // LANE, nd * rows_s, LANE), F32),
            pltpu.VMEM((cp, nlon), F32),
            pltpu.VMEM((cp, nlon), F32),
            pltpu.VMEM((jb, nlon, cp), F32),
            pltpu.VMEM((jb, nlon, cp), F32),
            ck.order_scratch(cp),
        ],
        compiler_params=params(62),
        name="grid_block",
    )(me, coef, xt, w_in, w_out, inv, inv_t, eye, gain, cmask, row_mask, *cots)
    return got[:n], got[n:]


def grid_final(ck, coef, xt, dh, me, fwd_t, eye, gain, cmask, row_mask, csh, n, cv):
    nd, _, rows_s, cp = coef.shape
    rows, nlon, _ = xt.shape
    step, mk = ck.step, ck.mk

    def body(me_ref, c_ref, xt_ref, dh_ref, ft_ref, eye_ref, g_ref, cm_ref, rm_ref, *refs):
        out_refs, (gg_ref, fin, oscr) = refs[:n], refs[n:]
        k = pl.program_id(1)
        at = pl.program_id(0) * ck.blocks + k

        @pl.when(at == 0)
        def _():
            gg_ref[...] = jnp.zeros_like(gg_ref)

        @pl.when(k == 0)
        def _():
            for d in range(nd):
                spread(fin, d * rows_s, c_ref[d, 0])

        for i in range(step):
            du = mm(ft_ref[...], pick_rows(fin, k * ck.jb + ck.raw(i), nd * mk, ck.stride))
            x = xt_ref[i].astype(F32)
            r1 = lax.rsqrt(jnp.sum(x * x, axis=1, keepdims=True) / CH + EPS)
            gd = g_ref[...] * du
            proj = jnp.sum(x * gd, axis=1, keepdims=True) / CH
            res = dh_ref[i].astype(F32) + r1 * gd - x * (r1 * r1 * r1 * proj)
            res = (res * (cm_ref[...] * rm_ref[at * step + i])).astype(BF)
            gg_ref[...] += jnp.sum(du * x * r1, axis=0, keepdims=True)
            store_transposed(out_refs, ck.raw(i), res, me_ref[0], eye_ref[...], oscr, csh)

    rowmap = ck.row_map(0, 0)
    got = pl.pallas_call(
        body,
        grid=ck.grid,
        in_specs=[
            SMEM,
            ck.coef_spec(rows_s, cp),
            pl.BlockSpec((step, nlon, cp), rowmap),
            pl.BlockSpec((step, nlon, cp), rowmap),
            whole(fwd_t.shape),
            whole(eye.shape),
            whole(gain.shape),
            whole(cmask.shape),
            SMEM,
        ],
        out_specs=[pl.BlockSpec((step, cv, nlon), rowmap)] * n
        + [pl.BlockSpec((1, cp), lambda s, k: (0, 0))],
        out_shape=[jax.ShapeDtypeStruct((rows, cv, nlon), BF)] * n
        + [jax.ShapeDtypeStruct((1, cp), F32)],
        scratch_shapes=[
            pltpu.VMEM((cp // LANE, nd * rows_s, LANE), F32),
            pltpu.VMEM((cp, nlon), F32),
        ],
        compiler_params=params(48),
        name="grid_final",
    )(me, coef, xt, dh, fwd_t, eye, gain, cmask, row_mask)
    return got[:n], got[n]


def adamw(param, grad, first, second, rate, decay):
    new_first = 0.5 * first + 0.5 * grad
    new_second = 0.5 * second + 0.5 * grad * grad
    update = new_first / BIAS_FIX / (jnp.sqrt(new_second / BIAS_FIX) + ADAM_EPS)
    return (param - rate * (update + decay * param), new_first, new_second)


def swap(value, axis):
    return lax.all_to_all(value, axis, split_axis=0, concat_axis=0, tiled=True)


def after(value, *others):
    return lax.optimization_barrier((value, others))[0]


def local(
    n_sp, n_tp,
    state, cotangent, rollout_lengths, channel_sizes, owner_slots,
    master, first_moment, second_moment, gains, gain_first, gain_second,
):
    slots, latd, flat = state.shape
    own, csh, cp = master.shape
    nlon = flat // csh
    sp, tp = lax.axis_index("sp"), lax.axis_index("tp")
    me = tp.astype(jnp.int32).reshape(1)
    degrees = owner_slots.shape[0] - 4
    n_mi = (degrees + n_sp - 1) // n_sp
    mpad = n_mi * n_sp
    plan = Plan(slots, latd, n_sp, n_tp, n_mi)
    chunks = plan.chunks
    nlatp = latd * n_sp
    valid = CVALID * nlon
    tile = 19 * 128
    lanes = pl.cdiv(valid, tile) * tile

    fwd, inv, analysis, synthesis = tables(NLAT, nlatp, nlon, degrees, mpad)
    fwd_t, inv_t = jnp.asarray(fwd.T), jnp.asarray(inv.T)
    fwd, inv = jnp.asarray(fwd), jnp.asarray(inv)
    eye = jnp.asarray(np.eye(nlon).astype(ml_dtypes.bfloat16))
    pick = (owner_slots[:degrees, None] == jnp.arange(n_sp * own)[None, :]).astype(BF)
    mine = lambda t: lax.dynamic_slice_in_dim(jnp.asarray(t), sp * n_mi, n_mi, 0)
    by_slot = lambda t: jnp.einsum("mlj,lq->mqj", mine(t), pick, preferred_element_type=F32).astype(BF)
    ana_q, syn_q = by_slot(analysis), by_slot(synthesis)
    ana_j, syn_j = jnp.swapaxes(ana_q, 1, 2), jnp.swapaxes(syn_q, 1, 2)

    def table(ck, t):
        return t if ck.nm == n_mi else lax.dynamic_slice_in_dim(t, tp * ck.nm, ck.nm, 0)

    chan = jnp.arange(cp)
    cmask = (chan % csh < channel_sizes[chan // csh]).astype(F32)
    rmask = (jnp.arange(csh) < channel_sizes[tp]).astype(F32)
    cmask2 = cmask[None, :]
    samples = rollout_lengths.shape[0]
    row_masks, cot_masks = [], []
    for ck in chunks:
        first, lat0 = (n_tp * plan.main, tp * ck.jn) if ck.left else (tp * plan.main, 0)
        ids = first + jnp.arange(ck.each)
        live = ids % ROLL < rollout_lengths[jnp.minimum(ids // ROLL, samples - 1)]
        live = (live & (ids < slots)).astype(F32)
        lat = (sp * latd + lat0 + jnp.arange(ck.jn) < NLAT).astype(F32)
        masks = jnp.ones((ck.each, 1), F32) * lat[None, :], live[:, None] * lat[None, :]
        masks = [(m.T if ck.left else m).reshape(-1) for m in masks]
        row_masks.append(masks[0])
        cot_masks.append(masks[1])

    copies = (master * (rmask[:, None] * cmask2)[None]).astype(BF)
    hrow = (jnp.arange(2 * csh) < 2 * channel_sizes[tp]).astype(F32).reshape(2, csh)
    raw = []
    for i in range(4):
        at = owner_slots[degrees + i] - sp * own
        inside = (at >= 0) & (at < own)
        piece = lax.dynamic_index_in_dim(master, jnp.clip(at, 0, own - 1), 0, keepdims=False)
        keep = hrow[i % 2][:, None] * cmask2 * inside.astype(F32)
        raw.append((piece * keep).astype(BF))
    gains_all = swap(jnp.broadcast_to(gains[None], (n_tp,) + gains.shape), "tp")
    gains_all = jnp.swapaxes(gains_all, 0, 1).reshape(2, cp)

    cut = lambda a: a[:, :valid].reshape(-1, CVALID, nlon)
    flat_of = lambda a: jnp.pad(a.reshape(a.shape[0], valid), ((0, 0), (0, lanes - valid)))
    send = lambda a, d: lax.ppermute(a, "tp", [(i, i ^ d) for i in range(n_tp)]) if d else a
    send_all = lambda arrays: [send(a, d) for d, a in enumerate(arrays)]
    rows3 = lambda v: v.reshape(v.shape[0], -1, cp)

    turn = []

    def swap_next(value, axes, *ties):
        out = swap(after(value, *turn, *ties), axes)
        turn[:] = [out]
        return out

    main, left = pack_rows(state, me, plan, lanes, tile)
    main = send_all(after(main, gains_all))
    left = send_all(after(left, main[1])) if left else []
    main, left = [cut(a) for a in main], [cut(a) for a in left]
    x5 = [main, left]
    spec_w = lax.all_gather(after(copies[:, :CROWS], main, gains_all), "tp", axis=0, tiled=False)
    gain_a, gain_b = gains_all[:1], gains_all[1:]
    n = len(chunks)
    odd = lambda arrays: [send(a, d) if d % 2 else a for d, a in enumerate(arrays)]
    even = lambda arrays: [a if d % 2 else send(a, d) for d, a in enumerate(arrays)]

    fs, xts = [], []
    for i, ck in enumerate(chunks):
        f, xt = fourier(ck, x5[i], me, fwd, eye, gain_a, cmask2, row_masks[i], csh)
        xts.append(xt)
        if i == 1:
            fs[0] = after(fs[0], f)
        fs.append(swap_next(rows3(f), ck.axes))
    dense = lax.psum_scatter(after(jnp.stack(raw), fs[0]), "sp", scatter_dimension=1, tiled=True)
    coefs = []
    for f, ck in zip(fs, chunks):
        c = legendre(ck, f, table(ck, ana_q), n_sp, False, "analysis")
        coefs.append(swap_next(c, "sp", *((spec_w,) if ck.left else ())))
    coefs[0] = after(coefs[0], dense)
    dense = lax.all_gather(after(dense, coefs[0]), "tp", axis=1, tiled=False)
    m, a = mix(chunks[0], coefs[0], spec_w, csh, NT, "mix_forward")
    mixed, coef_q = [swap_next(m, "sp")], [a]
    main, left = pack_rows(after(cotangent, m, dense), me, plan, lanes, tile)
    ahead = odd(main)
    if n > 1:
        m, a = mix(chunks[1], after(coefs[1], main), spec_w, csh, NT, "mix_forward")
        mixed.append(swap_next(m, "sp", ahead))
        coef_q.append(a)
    dense = lax.all_gather(after(dense, mixed[0]), "sp", axis=2, tiled=True)
    w_in = dense[:2].reshape(2 * cp, cp)
    w_out = dense[2:].reshape(2 * cp, cp)
    main, left = after((ahead, left), mixed[0])
    main, left = even(main), send_all(left)
    cots = [cut(ahead[d]) if d % 2 or d == 0 else cut(a) for d, a in enumerate(main)]
    if n > 1:
        mixed[1] = after(mixed[1], [c for d, c in enumerate(cots) if d % 2 or d == 0])
    synth = []
    for i, ck in enumerate(chunks):
        g = legendre(ck, mixed[i], table(ck, syn_j), ck.nd, True, "synthesis")
        synth.append(ck.grid_coef(swap_next(g, ck.axes, *((main, left) if i else ()))))
    cot5 = [cots, [cut(a) for a in left]]
    outs, rest, dgs = [], [], []
    for i, ck in enumerate(chunks):
        o, r = grid_block(
            ck, synth[i], xts[i], cot5[i], me, w_in, w_out, inv, inv_t, eye, gain_b, cmask2,
            cot_masks[i], csh,
        )
        outs.append([flat_of(a) for a in o])
        rest.append(r)
        if i == 0:
            dgs.append(swap_next(rows3(r[0]), ck.axes))
            main = odd(outs[0])
        else:
            dgs.append(swap_next(rows3(r[0]), ck.axes, main))
    left = outs[1] if n > 1 else []
    dbs = []
    for i, ck in enumerate(chunks):
        g = legendre(ck, dgs[i], table(ck, syn_q), n_sp, False, "synthesis_back")
        if i == 0:
            main, left = after((main, left), g)
            main, left = even(main), send_all(left)
            dbs.append(swap_next(g, "sp"))
        else:
            dbs.append(swap_next(g, "sp", main))
    das, grad_q = [], []
    for ck, b in zip(chunks, dbs):
        a, g = mix(ck, b, spec_w, csh, NN, "mix_backward")
        das.append(swap_next(a, "sp", *((left,) if ck.left else ())))
        grad_q.append(g)
    pieces_out = [(0, main)] + ([(-1, left)] if left else [])
    result = unpack_rows(pieces_out, me, plan, flat, valid, lanes, tile)
    half = own // 2
    dws_a = weight_grads(grad_q, coef_q, n_tp, CROWS, 0, half)
    dws_b = weight_grads(grad_q, coef_q, n_tp, CROWS, half, own - half)
    das[0] = after(das[0], dws_a, dws_b)
    dfs = []
    for ck, a in zip(chunks, das):
        g = legendre(ck, a, table(ck, ana_j), ck.nd, True, "analysis_back")
        dfs.append(swap_next(g, ck.axes))
    scatter = lambda v: lax.psum_scatter(v, "tp", scatter_dimension=0, tiled=False)
    spec_a = scatter(after(dws_a, pieces_out))
    dfs[0] = after(dfs[0], spec_a)
    spec_b = scatter(after(dws_b, spec_a))
    dfs[-1] = after(dfs[-1], spec_b)
    spec_g = jnp.concatenate([spec_a, spec_b], axis=0)
    pieces, gg_a = [], 0.0
    for i, ck in enumerate(chunks):
        o, gg = grid_final(
            ck, ck.grid_coef(dfs[i]), xts[i], rest[i][1], me, fwd_t, eye, gain_a, cmask2,
            row_masks[i], csh, n_tp, CVALID,
        )
        gg_a = gg_a + gg
        pieces.append((-1 if ck.left else 0, send_all([flat_of(a) for a in o])))

    dwi = sum(r[2] for r in rest)
    dwo = sum(r[3] for r in rest)
    gg_b = sum(r[4] for r in rest)
    dense_g = jnp.stack([dwi, dwo]).reshape(4, n_tp, csh, cp).astype(BF)
    dense_g = lax.psum_scatter(after(dense_g, dgs[0]), "sp", scatter_dimension=2, tiled=True)
    dense_g = lax.psum_scatter(after(dense_g, das[0]), "tp", scatter_dimension=1, tiled=False)
    dense_g = lax.all_gather(after(dense_g, dfs[0]), "sp", axis=1, tiled=True).astype(F32)
    spec_g = jnp.pad(spec_g.astype(F32), ((0, 0), (0, csh - CROWS), (0, 0)))
    grads = spec_g
    for i in range(4):
        hit = (owner_slots[degrees + i] == sp * own + jnp.arange(own))[:, None, None]
        grads = jnp.where(hit, dense_g[i][None], grads)
    new_master, new_first, new_second = adamw(master, grads, first_moment, second_moment, 0.03, 0.01)
    gain_g = lax.psum(after(jnp.concatenate([gg_a, gg_b], axis=0), new_master), ("sp", "tp"))
    gain_g = lax.dynamic_slice_in_dim(gain_g, tp * csh, csh, 1)
    new_gains, gain_one, gain_two = adamw(gains, gain_g, gain_first, gain_second, 0.5, 0.0)
    grad_state = unpack_rows(
        pieces, after(me, new_gains, new_master), plan, flat, valid, lanes, tile
    )
    return (
        result, grad_state, new_master, new_master.astype(BF), new_first, new_second,
        new_gains, gain_one, gain_two,
    )


def solution(mesh):
    wide, slot, gain = P(None, "sp", "tp"), P("sp", "tp", None), P(None, "tp")
    return jax.shard_map(
        functools.partial(local, mesh.shape["sp"], mesh.shape["tp"]),
        mesh=mesh,
        in_specs=(wide, wide, P(), P(), P(), slot, slot, slot, gain, gain, gain),
        out_specs=(wide, wide, slot, slot, slot, slot, gain, gain, gain),
        check_vma=False,
    )
```
